1024 devices in a mesh: group: 16 (over z), local: 64 (over y, x, core).
Axes of the slice: x: 4, y: 8, z: 16, core: 2. Of those that a mesh axis runs over, the one named last changes fastest.
Arguments:
- grad_out: bfloat16 [2048, 7168], P('group', 'local'), may hold values from -4 to 4
- routes: int32 [2048, 8], P('group'), may hold values from 0 to 127, as said below
- slots: int32 [2048, 8], P('group'), may hold values from 0 to 15, as said below
- gates: bfloat16 [2048, 8], P('group'), may hold values from 0.049804688 to 0.59765625
- w_down: bfloat16 [1024, 1024, 896], P(('group', 'local')), may hold values from -0.1875 to 0.1875
- saved_gate: bfloat16 [1024, 256, 128], P(('group', 'local')), may hold values from -5 to 5
- saved_up: bfloat16 [1024, 256, 128], P(('group', 'local')), may hold values from -5 to 5
Outputs:
- grad_gate_pre: bfloat16 [1024, 256, 128], P(('group', 'local'))
- grad_up_pre: bfloat16 [1024, 256, 128], P(('group', 'local'))
- grad_gates: float32 [2048, 8], P('group')
The draws below stay inside these ranges and needn't reach their ends.
Inputs may be any that keep to these rules, and one draw needn't show every extreme that they name: `routes`: each row names 8 different experts that lie in at most 4 groups of 8 consecutive experts. Among the tokens of one group index, no expert is named more than 16 times, and one expert is named exactly 16 times by the tokens of every group index. For one group index and one expert, the slots of the routes that name it are distinct and run from 0 without gaps.
All inputs are finite; a program needn't handle non-finite values.
Results may differ from the reference program's by a relative error of at most 0.0014.
Values may be sent and summed in bfloat16 or wider, within the bound.
No kernel may reach another device: no remote copies, remote signals or barrier semaphores. Data moves between devices by JAX's collectives and lax.ppermute only.
A program may use at most 32 MiB of HBM per device.

```python
import jax
import jax.numpy as jnp
from jax import lax

D = 7168
HID = 1024
EXP_GRP = 8
TOPK = 8
TOPG = 4
TOK_GRP = 128
N_SHARD = 8
D_SH = 896
HID_SH = 128
SLOTS = 16
CAP = 256
EXPERTS = 128
TOKENS = 2048
N_GROUP = 16


def route_table(key):
    column_tokens = TOK_GRP
    expert_ids = jnp.arange(EXPERTS, dtype=jnp.int32)
    group_index = jnp.arange(N_GROUP, dtype=jnp.int32)
    popular = jax.random.randint(jax.random.fold_in(key, 11), (EXPERTS,), 0, 4) * 262144
    leader = jax.random.randint(jax.random.fold_in(key, 12), (), 0, EXPERTS)
    popular = popular + jnp.where(expert_ids == leader, 2097152, 0)

    def column(column_key):
        first_key, second_key, third_key = jax.random.split(column_key, 3)
        favored = jax.random.randint(first_key, (), 0, EXPERTS)
        jitter = jax.random.randint(second_key, (column_tokens, EXPERTS), 0, 262144)
        visit_order = jax.random.permutation(third_key, column_tokens)
        base_value = popular + jnp.where(expert_ids == favored, 1048576, 0)

        def assign(state_tuple, position):
            counts, chosen_rows, places = state_tuple
            token_row = visit_order[position]
            priority = base_value + jitter[token_row]
            usable = counts < SLOTS
            usable_groups = jnp.sum(usable.reshape(N_GROUP, EXP_GRP).astype(jnp.int32), axis=1)
            best_value = jnp.max(jnp.where(usable, priority, 0).reshape(N_GROUP, EXP_GRP), axis=1)
            group_score = (jnp.minimum(usable_groups, 2) * 8388608 + best_value) * N_GROUP + group_index
            chosen_groups = lax.top_k(group_score, TOPG)[1]
            in_chosen = jnp.any(group_index[:, None] == chosen_groups[None, :], axis=1)
            in_chosen = jnp.repeat(in_chosen, EXP_GRP)
            expert_score = jnp.where(in_chosen & usable, priority * EXPERTS + expert_ids, expert_ids - EXPERTS)
            picked = lax.top_k(expert_score, TOPK)[1].astype(jnp.int32)
            placed = counts[picked]
            counts = counts + jnp.sum((picked[:, None] == expert_ids[None, :]).astype(jnp.int32), axis=0)
            chosen_rows = chosen_rows.at[token_row].set(picked)
            places = places.at[token_row].set(placed)
            return ((counts, chosen_rows, places), None)
        initial = (jnp.zeros((EXPERTS,), jnp.int32), jnp.zeros((column_tokens, TOPK), jnp.int32), jnp.zeros((column_tokens, TOPK), jnp.int32))
        outcome = lax.scan(assign, initial, jnp.arange(column_tokens))[0]
        return (outcome[1], outcome[2])
    tables, places = jax.vmap(column)(jax.random.split(jax.random.fold_in(key, 13), N_GROUP))
    return (tables.reshape(TOKENS, TOPK), places.reshape(TOKENS, TOPK))


def draw_routes(key, part):
    return route_table(key)[0]


def draw_slots(key, part):
    return route_table(key)[1]


def steps_of(key, extent, shards, least, top_value):
    def one(axis_at, parts):
        heights = jax.random.uniform(jax.random.fold_in(jax.random.fold_in(key, 6), axis_at), (parts,), jnp.float32, least / len(shards), top_value / len(shards))
        return jnp.repeat(jnp.exp(heights), extent[axis_at] // parts).reshape((-1,) + (1,) * (len(extent) - axis_at - 1))

    level = one(*shards[0])
    for cut in shards[1:]:
        level = level * one(*cut)
    return level


def bell_draw(own_key, dims, spread, limit, shards=(), held_as=jnp.bfloat16):
    level = steps_of(own_key, dims, shards, -0.22, 0.18) if shards else 1.0
    array = jax.random.normal(own_key, dims, jnp.float32) * spread * level
    return jnp.minimum(jnp.maximum(array, -limit), limit).astype(held_as)


def setup_inputs(seed: int = 0) -> dict:
    streams_of = jax.random.split(jax.random.key(seed), 8)
    return {
        "grad_out": bell_draw(streams_of[0], (TOKENS, D), 0.3, 4.0, ((0, 16), (1, 64))),
        "routes": draw_routes(jax.random.fold_in(streams_of[7], 71), 0),
        "slots": draw_slots(jax.random.fold_in(streams_of[7], 71), 0),
        "gates": jnp.clip(0.049804688 + 0.54785156 * jax.random.uniform(streams_of[3], (TOKENS, TOPK), jnp.float32) ** steps_of(streams_of[3], (TOKENS, TOPK), ((0, 16),), -0.2, 0.2), 0.049804688, 0.59765625).astype(jnp.bfloat16),
        "w_down": bell_draw(streams_of[4], (EXPERTS * N_SHARD, HID, D_SH), HID ** -0.5, 0.1875, ((0, 1024),)),
        "saved_gate": bell_draw(streams_of[5], (EXPERTS * N_SHARD, CAP, HID_SH), 0.7, 5.0, ((0, 1024),)),
        "saved_up": bell_draw(streams_of[6], (EXPERTS * N_SHARD, CAP, HID_SH), 0.7, 5.0, ((0, 1024),)),
    }


def expert_major(values_in, tail_shape):
    shaped = values_in.reshape((N_GROUP, N_SHARD, EXP_GRP) + tail_shape)
    return jnp.transpose(shaped, (0, 2, 1, 3, 4)).reshape((EXPERTS, N_SHARD) + tail_shape)


def device_major(values_in, tail_shape):
    shaped = values_in.reshape((N_GROUP, EXP_GRP, N_SHARD) + tail_shape)
    return jnp.transpose(shaped, (0, 2, 1, 3, 4)).reshape((EXPERTS * N_SHARD,) + tail_shape)


def reference(grad_out, routes, slots, gates, w_down, saved_gate, saved_up):
    token_ids = jnp.arange(TOKENS, dtype=jnp.int32)
    source_group = token_ids // TOK_GRP
    places = (source_group[:, None] * SLOTS + slots).astype(jnp.int32)
    flat_experts = routes.reshape(-1).astype(jnp.int32)
    flat_places = places.reshape(-1)
    slot_source = jnp.full((EXPERTS, CAP), TOKENS, jnp.int32).at[flat_experts, flat_places].set(jnp.repeat(token_ids, TOPK))
    slot_gate = jnp.zeros((EXPERTS, CAP), jnp.float32).at[flat_experts, flat_places].set(gates.reshape(-1).astype(jnp.float32))
    padded = jnp.concatenate([grad_out, jnp.zeros((1, D), grad_out.dtype)], axis=0)
    weight_view = expert_major(w_down, (HID, D_SH))
    gate_view = expert_major(saved_gate, (CAP, HID_SH))
    up_view = expert_major(saved_up, (CAP, HID_SH))

    def per_expert(operands):
        source_ids, gate_values, weight_blocks, gate_blocks, up_blocks = operands
        dispatched = padded[source_ids]
        weight = jnp.transpose(weight_blocks, (1, 0, 2)).reshape(HID, D)
        hidden_grad = jnp.dot(dispatched, weight.T, preferred_element_type=jnp.float32)
        gate_pre = jnp.transpose(gate_blocks, (1, 0, 2)).reshape(CAP, HID).astype(jnp.float32)
        up_pre = jnp.transpose(up_blocks, (1, 0, 2)).reshape(CAP, HID).astype(jnp.float32)
        sigmoid_gate = jax.nn.sigmoid(gate_pre)
        hidden = gate_pre * sigmoid_gate * up_pre
        route_terms = jnp.sum(hidden_grad * hidden, axis=1)
        scaled = gate_values[:, None] * hidden_grad
        grad_up = (scaled * gate_pre * sigmoid_gate).astype(jnp.bfloat16)
        grad_gate = (scaled * up_pre * sigmoid_gate * (1.0 + gate_pre * (1.0 - sigmoid_gate))).astype(jnp.bfloat16)
        grad_gate = jnp.transpose(grad_gate.reshape(CAP, N_SHARD, HID_SH), (1, 0, 2))
        grad_up = jnp.transpose(grad_up.reshape(CAP, N_SHARD, HID_SH), (1, 0, 2))
        return grad_gate, grad_up, route_terms

    grad_gate_pre, grad_up_pre, route_terms = lax.map(per_expert, (slot_source, slot_gate, weight_view, gate_view, up_view))
    grad_gates = route_terms[routes, places]
    grad_gate_pre = device_major(grad_gate_pre, (CAP, HID_SH))
    grad_up_pre = device_major(grad_up_pre, (CAP, HID_SH))
    return grad_gate_pre, grad_up_pre, grad_gates
```

```python
import jax
import jax.numpy as jnp
from jax import lax
from jax.experimental import pallas as pl
from jax.experimental.pallas import tpu as pltpu
from jax.sharding import Mesh, PartitionSpec as P

EXP_GRP = 8
NT = (((1,), (1,)), ((), ()))
F32 = jnp.float32
BF16 = jnp.bfloat16


def lanes(shape):
    return lax.broadcasted_iota(jnp.int32, shape, len(shape) - 1)


def rows(shape):
    return lax.broadcasted_iota(jnp.int32, shape, 0)


def dispatch_kernel(where_ref, tokens_ref, routes_ref, slots_ref, gates_ref, out_ref, gate_ref):
    groups, _, lane_count = out_ref.shape
    tok_count = tokens_ref.shape[1]
    slot_count = 16
    capacity = groups * slot_count
    expert = where_ref[0]
    routes = routes_ref[...]
    place = jnp.where(
        routes % EXP_GRP == expert, routes // EXP_GRP * slot_count + slots_ref[...], -1
    )
    row_ids = rows((capacity, tok_count))
    pick = jnp.zeros((capacity, tok_count), F32)
    gate = jnp.zeros((capacity, tok_count), F32)
    for k in range(routes.shape[0]):
        hit = row_ids == place[k : k + 1, :]
        pick = jnp.where(hit, 1.0, pick)
        gate = jnp.where(hit, gates_ref[k : k + 1, :], gate)
    pick = pick.astype(BF16)
    for b in range(tokens_ref.shape[0] // lane_count):
        block = lax.dot_general(
            pick,
            tokens_ref[b * lane_count : (b + 1) * lane_count, :],
            NT,
            preferred_element_type=F32,
        )
        out_ref[:, b * slot_count : (b + 1) * slot_count, :] = block.astype(BF16).reshape(
            groups, slot_count, lane_count
        )
    gate_ref[...] = jnp.broadcast_to(
        jnp.sum(gate, axis=1, keepdims=True), (capacity, lane_count)
    )


def hidden_kernel(gate_ref, up_ref, out_ref):
    gate_pre = gate_ref[...].astype(F32)
    out_ref[...] = gate_pre * jax.nn.sigmoid(gate_pre) * up_ref[...].astype(F32)


def matmul_kernel(where_ref, rows_ref, w_ref, hidden_ref, gate_ref, give_ref, *outs):
    keep_refs, term_ref = outs[:-1], outs[-1]
    groups, _, lane_count = rows_ref.shape
    slot_count = 16
    capacity = groups * slot_count
    group, shard = where_ref[0], where_ref[1]
    own, quad = shard % 2, shard // 2
    blocks = w_ref.shape[1] // lane_count
    x = jnp.concatenate(
        [
            rows_ref[:, b * slot_count : (b + 1) * slot_count, :].reshape(capacity, lane_count)
            for b in range(blocks)
        ],
        axis=1,
    )
    terms = jnp.zeros((capacity, lane_count), F32)
    for d in range(4):
        for mine in (0, 1):
            target = (quad + d) % 4 * 2 + (own if mine else 1 - own)
            part = lax.dot_general(
                x,
                w_ref[pl.ds(pl.multiple_of(target * lane_count, lane_count), lane_count), :],
                NT,
                preferred_element_type=F32,
            )
            terms += part * hidden_ref[target]
            if mine:
                keep_refs[d][...] = part
            else:
                give_ref[d] = part
    total = jnp.sum(terms, axis=1, keepdims=True)
    row_ids, lane_ids = rows((capacity, lane_count)), lanes((capacity, lane_count))
    hit = lane_ids == group % 8 * slot_count + row_ids % slot_count
    pads = jnp.zeros((groups, 6, lane_count), F32)
    term = jnp.sum(
        jnp.where(hit, total, 0.0).reshape(groups, slot_count, lane_count), axis=1, keepdims=True
    )
    gate = jnp.sum(
        jnp.where(hit, gate_ref[...], 0.0).reshape(groups, slot_count, lane_count),
        axis=1,
        keepdims=True,
    )
    term_ref[...] = jnp.concatenate([term, gate, pads], axis=1)


def output_kernel(h0, h1, h2, h3, home_ref, gate_pre_ref, up_pre_ref, grad_gate_ref, grad_up_ref):
    hidden_grad = h0[...] + h1[...] + h2[...] + h3[...]
    capacity, lane_count = hidden_grad.shape
    groups = home_ref.shape[0]
    gates = jnp.broadcast_to(
        home_ref[:, 1:2, :], (groups, capacity // groups, lane_count)
    ).reshape(capacity, lane_count)
    hit = lanes((capacity, lane_count)) == rows((capacity, lane_count)) % lane_count
    gate = jnp.sum(jnp.where(hit, gates, 0.0), axis=1, keepdims=True)
    gate_pre = gate_pre_ref[...].astype(F32)
    up_pre = up_pre_ref[...].astype(F32)
    sigmoid_gate = jax.nn.sigmoid(gate_pre)
    scaled = gate * hidden_grad
    grad_up_ref[...] = (scaled * gate_pre * sigmoid_gate).astype(BF16)
    grad_gate_ref[...] = (
        scaled * up_pre * sigmoid_gate * (1.0 + gate_pre * (1.0 - sigmoid_gate))
    ).astype(BF16)


def collect_kernel(terms_ref, routes_ref, slots_ref, out_ref):
    shards, experts, halves, lane_count = terms_ref.shape
    tok_count, route_count = routes_ref.shape
    table = terms_ref[0]
    for s in range(1, shards):
        table += terms_ref[s]
    routes = routes_ref[...]
    place = routes // EXP_GRP * 16 + slots_ref[...]
    expert = routes % EXP_GRP
    out = jnp.zeros((tok_count, route_count), F32)
    route_ids = lanes((tok_count, route_count))
    expert_ids = lanes((tok_count, experts))
    for k in range(route_count):
        picked = jnp.zeros((tok_count, experts), F32)
        for h in range(halves):
            hit = lanes((tok_count, lane_count)) + h * lane_count == place[:, k : k + 1]
            picked += lax.dot_general(
                jnp.where(hit, 1.0, 0.0),
                table[:, h, :],
                NT,
                preferred_element_type=F32,
                precision=lax.Precision.HIGHEST,
            )
        column = jnp.sum(
            jnp.where(expert_ids == expert[:, k : k + 1], picked, 0.0), axis=1, keepdims=True
        )
        out = jnp.where(route_ids == k, column, out)
    out_ref[...] = out


VMEM = pl.BlockSpec(memory_space=pltpu.VMEM)
SMEM = pl.BlockSpec(memory_space=pltpu.SMEM)


def call(kernel, specs, out_shape, *args):
    outs = jax.tree.map(lambda _: VMEM, out_shape)
    return pl.pallas_call(
        kernel,
        in_specs=specs,
        out_specs=outs,
        out_shape=out_shape,
        compiler_params=pltpu.CompilerParams(vmem_limit_bytes=24 << 20),
    )(*args)


def shards(grad_out, routes, slots, gates, w_down, saved_gate, saved_up):
    groups = lax.axis_size("group")
    shard_count = lax.axis_size("y")
    capacity, lane_count = saved_gate.shape[1:]
    tok_count, col_width = grad_out.shape
    width = w_down.shape[2]
    group, shard, expert = (lax.axis_index(a) for a in ("group", "y", "xc"))
    where = jnp.stack([group, shard]).astype(jnp.int32)

    token_view = jnp.broadcast_to(grad_out.T[None], (EXP_GRP, col_width, tok_count))
    token_view = lax.all_to_all(token_view, "xc", 0, 0, tiled=True).reshape(width, tok_count)
    slot_rows = jax.ShapeDtypeStruct((groups, width // lane_count * 16, lane_count), BF16)
    column = jax.ShapeDtypeStruct((capacity, lane_count), F32)
    send, gate_rows = call(
        dispatch_kernel,
        [SMEM] + [VMEM] * 4,
        (slot_rows, column),
        expert.astype(jnp.int32)[None],
        token_view,
        routes.T,
        slots.T,
        gates.T.astype(F32),
    )

    pre = jnp.concatenate([saved_gate, saved_up], axis=0)
    send, pre = lax.optimization_barrier((send, pre))
    expert_rows = lax.all_to_all(send, "group", 0, 0, tiled=True)
    every_pre = lax.all_gather(pre, "y")
    full = jax.ShapeDtypeStruct((shard_count, capacity, lane_count), F32)
    hidden = call(hidden_kernel, [VMEM] * 2, full, every_pre[:, 0], every_pre[:, 1])

    give, k0, k1, k2, k3, terms = call(
        matmul_kernel,
        [SMEM] + [VMEM] * 4,
        (
            jax.ShapeDtypeStruct((4, capacity, lane_count), F32),
            column,
            column,
            column,
            column,
            jax.ShapeDtypeStruct((groups, 8, lane_count), F32),
        ),
        where,
        expert_rows,
        w_down[0],
        hidden,
        gate_rows,
    )

    got = lax.ppermute(give, "y", [(i, i ^ 1) for i in range(shard_count)])
    home = lax.all_to_all(terms, "group", 0, 0, tiled=True)
    parts = [k + got[d] for d, k in enumerate((k0, k1, k2, k3))]
    for d in (2, 1, 3):
        parts[d] = lax.ppermute(
            parts[d], "y", [(i, (i + 2 * d) % shard_count) for i in range(shard_count)]
        )
    own_terms = jnp.sum(home[:, 0, :].reshape(2, groups // 2, lane_count), axis=1)
    every_term = lax.all_to_all(
        jnp.broadcast_to(own_terms[None], (shard_count * EXP_GRP, 2, lane_count)),
        ("y", "xc"),
        0,
        0,
        tiled=True,
    ).reshape(shard_count, EXP_GRP, 2, lane_count)
    out = jax.ShapeDtypeStruct((capacity, lane_count), BF16)
    grad_gate, grad_up = call(
        output_kernel, [VMEM] * 7, (out, out), *parts, home, saved_gate[0], saved_up[0]
    )
    grad_gates = call(
        collect_kernel,
        [VMEM] * 3,
        jax.ShapeDtypeStruct(routes.shape, F32),
        every_term,
        routes,
        slots,
    )
    return (grad_gate[None], grad_up[None], grad_gates)


def solution(mesh):
    fine = Mesh(mesh.devices.reshape(mesh.shape["group"], -1, EXP_GRP), ("group", "y", "xc"))
    local, device = ("y", "xc"), ("group", "y", "xc")
    return jax.shard_map(
        shards,
        mesh=fine,
        in_specs=(
            P("group", local),
            P("group", None),
            P("group", None),
            P("group", None),
            P(device, None, None),
            P(device, None, None),
            P(device, None, None),
        ),
        out_specs=(P(device, None, None), P(device, None, None), P("group", None)),
        check_vma=False,
    )
```

```python
import jax
import jax.numpy as jnp
from jax import lax
from jax.experimental import pallas as pl
from jax.experimental.pallas import tpu as pltpu
from jax.sharding import Mesh, PartitionSpec as P

EXP_GRP = 8
SLOTS = 16
PAD = 8
NT = (((1,), (1,)), ((), ()))
TN = (((0,), (0,)), ((), ()))
F32 = jnp.float32
BF16 = jnp.bfloat16


def lanes(shape):
    return lax.broadcasted_iota(jnp.int32, shape, len(shape) - 1)


def rows(shape):
    return lax.broadcasted_iota(jnp.int32, shape, 0)


def dispatch_kernel(tokens_ref, routes_ref, slots_ref, gates_ref, out_ref):
    col_width, tok_count = tokens_ref.shape
    lane_count = out_ref.shape[2]
    place = routes_ref[...] * SLOTS + slots_ref[...]
    gates = gates_ref[...].astype(F32)
    spare = (lane_count - col_width, tok_count)
    features = jnp.concatenate([tokens_ref[...], jnp.zeros(spare, BF16)], axis=0)
    marks = jnp.where(rows((lane_count, tok_count)) == col_width, 1.0, 0.0).astype(BF16)
    source = jnp.concatenate([features, marks], axis=1)
    chunk = 256
    for start in range(0, out_ref.shape[0] * SLOTS, chunk):
        row_ids = rows((chunk, tok_count)) + start
        pick = jnp.zeros((chunk, tok_count), F32)
        gate = jnp.zeros((chunk, tok_count), F32)
        for k in range(place.shape[0]):
            hit = row_ids == place[k : k + 1, :]
            pick = jnp.where(hit, 1.0, pick)
            gate = jnp.where(hit, gates[k : k + 1, :], gate)
        both = jnp.concatenate([pick.astype(BF16), gate.astype(BF16)], axis=1)
        block = lax.dot_general(both, source, NT, preferred_element_type=F32)
        out_ref[start // SLOTS : (start + chunk) // SLOTS] = block.astype(BF16).reshape(
            chunk // SLOTS, SLOTS, lane_count
        )


def hidden_kernel(gate_ref, up_ref, out_ref):
    gate_pre = gate_ref[...].astype(F32)
    out_ref[...] = gate_pre * jax.nn.sigmoid(gate_pre) * up_ref[...].astype(F32)


def matmul_kernel(shard_ref, rows_ref, w_ref, *refs):
    hidden_refs, (part_ref, gate_ref) = refs[:-2], refs[-2:]
    groups, parts, _, lane_count = rows_ref.shape
    capacity = groups * SLOTS
    col_width = w_ref.shape[1] // parts
    shard = shard_ref[0]
    count = part_ref.shape[0]
    blocks = [rows_ref[:, e].reshape(capacity, lane_count) for e in range(parts)]
    x = jnp.concatenate([b[:, :col_width] for b in blocks], axis=1)
    terms = jnp.zeros((capacity, lane_count), F32)
    for j in range(count):
        target = (shard + j) % count
        first = pl.multiple_of(target * lane_count, lane_count)
        part = lax.dot_general(
            x, w_ref[pl.ds(first, lane_count), :], NT, preferred_element_type=F32
        )
        terms += part * hidden_refs[j][...]
        part_ref[target, :capacity] = part
    total = jnp.sum(terms, axis=1, keepdims=True)
    hit = lanes((capacity, lane_count)) == rows((capacity, lane_count)) % lane_count
    halves = capacity // lane_count
    line = jnp.sum(jnp.where(hit, total, 0.0).reshape(halves, lane_count, lane_count), axis=1)
    line = jnp.concatenate([line, jnp.zeros((PAD - halves, lane_count), F32)], axis=0)
    for j in range(count):
        part_ref[j, capacity:] = line
    gate = jnp.where(lanes((capacity, lane_count)) == col_width, blocks[0].astype(F32), 0.0)
    gate_ref[...] = jnp.broadcast_to(
        jnp.sum(gate, axis=1, keepdims=True), (capacity, lane_count)
    )


def terms_kernel(part_ref, out_ref):
    total = part_ref[0]
    for s in range(1, part_ref.shape[0]):
        total += part_ref[s]
    devices, _, lane_count = out_ref.shape
    half = devices // 2
    out_ref[:half] = jnp.broadcast_to(total[0:1, :][None], (half, 1, lane_count))
    out_ref[half:] = jnp.broadcast_to(total[1:2, :][None], (half, 1, lane_count))


def output_kernel(part_ref, gate_ref, gate_pre_ref, up_pre_ref, grad_gate_ref, grad_up_ref):
    capacity = gate_ref.shape[0]
    hidden_grad = part_ref[0, :capacity]
    for s in range(1, part_ref.shape[0]):
        hidden_grad += part_ref[s, :capacity]
    gate_pre = gate_pre_ref[...].astype(F32)
    up_pre = up_pre_ref[...].astype(F32)
    sigmoid_gate = jax.nn.sigmoid(gate_pre)
    scaled = gate_ref[...] * hidden_grad
    grad_up_ref[...] = (scaled * gate_pre * sigmoid_gate).astype(BF16)
    grad_gate_ref[...] = (
        scaled * up_pre * sigmoid_gate * (1.0 + gate_pre * (1.0 - sigmoid_gate))
    ).astype(BF16)


def collect_kernel(group_ref, terms_ref, routes_ref, slots_ref, out_ref):
    experts, _, lane_count = terms_ref.shape
    route_count, tok_count = routes_ref.shape
    table = terms_ref[:, 0, :]
    offset = group_ref[0] % (lane_count // SLOTS) * SLOTS
    for k in range(route_count):
        hit = rows((experts, tok_count)) == routes_ref[k : k + 1, :]
        picked = lax.dot_general(
            table,
            jnp.where(hit, 1.0, 0.0),
            TN,
            preferred_element_type=F32,
            precision=lax.Precision.HIGHEST,
        )
        own = rows((lane_count, tok_count)) == slots_ref[k : k + 1, :] + offset
        out_ref[k : k + 1, :] = jnp.sum(jnp.where(own, picked, 0.0), axis=0, keepdims=True)


VMEM = pl.BlockSpec(memory_space=pltpu.VMEM)
SMEM = pl.BlockSpec(memory_space=pltpu.SMEM)


def call(kernel, specs, out_shape, *args):
    return pl.pallas_call(
        kernel,
        in_specs=specs,
        out_specs=jax.tree.map(lambda _: VMEM, out_shape),
        out_shape=out_shape,
        compiler_params=pltpu.CompilerParams(vmem_limit_bytes=24 << 20),
    )(*args)


def shards(grad_out, routes, slots, gates, w_down, saved_gate, saved_up):
    shape = jax.ShapeDtypeStruct
    groups, shard_count, parts = (lax.axis_size(a) for a in ("group", "y", "xc"))
    capacity, lane_count = saved_gate.shape[1:]
    group = lax.axis_index("group").astype(jnp.int32)[None]
    shard = lax.axis_index("y").astype(jnp.int32)[None]
    column = shape((capacity, lane_count), F32)

    send = call(
        dispatch_kernel,
        [VMEM] * 4,
        shape((groups * parts, SLOTS, lane_count), BF16),
        grad_out.T,
        routes.T,
        slots.T,
        gates.T,
    )
    send, gate_pre, up_pre = lax.optimization_barrier((send, saved_gate[0], saved_up[0]))
    expert_rows = lax.all_to_all(send, ("group", "xc"), 0, 0, tiled=True)

    hidden = call(hidden_kernel, [VMEM] * 2, column, gate_pre, up_pre)
    others = {
        j: lax.ppermute(
            hidden, "y", [(i, (i - j) % shard_count) for i in range(shard_count)]
        )
        for j in range(1, shard_count)
    }
    part, gate_rows = call(
        matmul_kernel,
        [SMEM] + [VMEM] * (2 + shard_count),
        (shape((shard_count, capacity + PAD, lane_count), F32), column),
        shard,
        expert_rows.reshape(groups, parts, SLOTS, lane_count),
        w_down[0],
        hidden,
        *(others[j] for j in range(1, shard_count)),
    )

    part = lax.all_to_all(part, "y", 0, 0, tiled=True)
    tail = pl.BlockSpec((shard_count, PAD, lane_count), lambda i: (0, capacity // PAD, 0))
    term_rows = pl.pallas_call(
        terms_kernel,
        grid=(1,),
        in_specs=[tail],
        out_specs=pl.BlockSpec((groups * parts, 1, lane_count), lambda i: (0, 0, 0)),
        out_shape=shape((groups * parts, 1, lane_count), F32),
    )(part)
    home_terms = lax.all_to_all(term_rows, ("group", "xc"), 0, 0, tiled=True)
    out = shape((capacity, lane_count), BF16)
    grad_gate, grad_up = call(
        output_kernel, [VMEM] * 4, (out, out), part, gate_rows, saved_gate[0], saved_up[0]
    )
    grad_gates = call(
        collect_kernel,
        [SMEM] + [VMEM] * 3,
        shape(routes.shape[::-1], F32),
        group,
        home_terms,
        routes.T,
        slots.T,
    )
    return (grad_gate[None], grad_up[None], grad_gates.T)


def solution(mesh):
    fine = Mesh(mesh.devices.reshape(mesh.shape["group"], -1, EXP_GRP), ("group", "y", "xc"))
    local, device = ("y", "xc"), ("group", "y", "xc")
    return jax.shard_map(
        shards,
        mesh=fine,
        in_specs=(
            P("group", local),
            P("group", None),
            P("group", None),
            P("group", None),
            P(device, None, None),
            P(device, None, None),
            P(device, None, None),
        ),
        out_specs=(P(device, None, None), P(device, None, None), P("group", None)),
        check_vma=False,
    )
```

```python
import jax
import jax.numpy as jnp
from jax import lax
from jax.experimental import pallas as pl
from jax.experimental.pallas import tpu as pltpu
from jax.sharding import Mesh, PartitionSpec as P

EXP_GRP = 8
SLOTS = 16
NT = (((1,), (1,)), ((), ()))
F32 = jnp.float32
BF16 = jnp.bfloat16


def lanes(shape):
    return lax.broadcasted_iota(jnp.int32, shape, len(shape) - 1)


def rows(shape):
    return lax.broadcasted_iota(jnp.int32, shape, 0)


def dispatch_kernel(tokens_ref, routes_ref, slots_ref, gates_ref, out_ref):
    col_width, tok_count = tokens_ref.shape
    lane_count = out_ref.shape[2]
    place = routes_ref[...] * SLOTS + slots_ref[...]
    gates = gates_ref[...].astype(F32)
    spare = (lane_count - col_width, tok_count)
    features = jnp.concatenate([tokens_ref[...], jnp.zeros(spare, BF16)], axis=0)
    marks = jnp.where(rows((lane_count, tok_count)) == col_width, 1.0, 0.0).astype(BF16)
    source = jnp.concatenate([features, marks], axis=1)
    chunk = 256
    for start in range(0, out_ref.shape[0] * SLOTS, chunk):
        row_ids = rows((chunk, tok_count)) + start
        pick = jnp.zeros((chunk, tok_count), F32)
        gate = jnp.zeros((chunk, tok_count), F32)
        for k in range(place.shape[0]):
            hit = row_ids == place[k : k + 1, :]
            pick = jnp.where(hit, 1.0, pick)
            gate = jnp.where(hit, gates[k : k + 1, :], gate)
        both = jnp.concatenate([pick.astype(BF16), gate.astype(BF16)], axis=1)
        block = lax.dot_general(both, source, NT, preferred_element_type=F32)
        out_ref[start // SLOTS : (start + chunk) // SLOTS] = block.astype(BF16).reshape(
            chunk // SLOTS, SLOTS, lane_count
        )


def hidden_kernel(gate_ref, up_ref, out_ref):
    gate_pre = gate_ref[...].astype(F32)
    out_ref[...] = gate_pre * jax.nn.sigmoid(gate_pre) * up_ref[...].astype(F32)


def matmul_kernel(where_ref, rows_ref, w_ref, same_ref, other_ref, give_ref, *outs):
    keep_refs, (term_ref, gate_ref) = outs[:-2], outs[-2:]
    groups, parts, _, lane_count = rows_ref.shape
    capacity = groups * SLOTS
    col_width = w_ref.shape[1] // parts
    group, shard = where_ref[0], where_ref[1]
    own, quad = shard % 2, shard // 2
    quads = give_ref.shape[0]
    blocks = [rows_ref[:, e].reshape(capacity, lane_count) for e in range(parts)]
    x = jnp.concatenate([b[:, :col_width] for b in blocks], axis=1)
    terms = jnp.zeros((capacity, lane_count), F32)
    for d in range(quads):
        target = (quad + d) % quads
        for mine, hidden_ref in ((0, other_ref), (1, same_ref)):
            unit = target * 2 + (own if mine else 1 - own)
            first = pl.multiple_of(unit * lane_count, lane_count)
            part = lax.dot_general(
                x, w_ref[pl.ds(first, lane_count), :], NT, preferred_element_type=F32
            )
            terms += part * hidden_ref[target]
            if mine:
                keep_refs[d][...] = part
            else:
                give_ref[d] = part
    total = jnp.sum(terms, axis=1, keepdims=True)
    row_ids, lane_ids = rows((capacity, lane_count)), lanes((capacity, lane_count))
    hit = lane_ids == group % (lane_count // SLOTS) * SLOTS + row_ids % SLOTS
    term_ref[...] = jnp.sum(
        jnp.where(hit, total, 0.0).reshape(groups, SLOTS, lane_count), axis=1, keepdims=True
    )
    gate = jnp.where(lane_ids == col_width, blocks[0].astype(F32), 0.0)
    gate_ref[...] = jnp.broadcast_to(
        jnp.sum(gate, axis=1, keepdims=True), (capacity, lane_count)
    )


def spread_kernel(home_ref, out_ref):
    groups, _, lane_count = home_ref.shape
    half = groups // 2
    home = jnp.sum(home_ref[...].reshape(2, half, lane_count), axis=1)
    out_ref[...] = jnp.broadcast_to(home[None], out_ref.shape)


def output_kernel(h0, h1, h2, h3, gate_ref, gate_pre_ref, up_pre_ref, grad_gate_ref, grad_up_ref):
    hidden_grad = h0[...] + h1[...] + h2[...] + h3[...]
    gate_pre = gate_pre_ref[...].astype(F32)
    up_pre = up_pre_ref[...].astype(F32)
    sigmoid_gate = jax.nn.sigmoid(gate_pre)
    scaled = gate_ref[...] * hidden_grad
    grad_up_ref[...] = (scaled * gate_pre * sigmoid_gate).astype(BF16)
    grad_gate_ref[...] = (
        scaled * up_pre * sigmoid_gate * (1.0 + gate_pre * (1.0 - sigmoid_gate))
    ).astype(BF16)


def collect_kernel(terms_ref, routes_ref, slots_ref, out_ref):
    shard_count, experts, halves, lane_count = terms_ref.shape
    route_count, tok_count = routes_ref.shape
    table = terms_ref[0]
    for s in range(1, shard_count):
        table += terms_ref[s]
    routes = routes_ref[...]
    place = routes // EXP_GRP * SLOTS + slots_ref[...]
    for k in range(route_count):
        picked = jnp.zeros((experts, tok_count), F32)
        for h in range(halves):
            hit = rows((lane_count, tok_count)) + h * lane_count == place[k : k + 1, :]
            picked += jnp.dot(
                table[:, h, :],
                jnp.where(hit, 1.0, 0.0),
                preferred_element_type=F32,
                precision=lax.Precision.HIGHEST,
            )
        own = rows((experts, tok_count)) == routes[k : k + 1, :] % EXP_GRP
        out_ref[k : k + 1, :] = jnp.sum(jnp.where(own, picked, 0.0), axis=0, keepdims=True)


VMEM = pl.BlockSpec(memory_space=pltpu.VMEM)
SMEM = pl.BlockSpec(memory_space=pltpu.SMEM)


def call(kernel, specs, out_shape, *args):
    return pl.pallas_call(
        kernel,
        in_specs=specs,
        out_specs=jax.tree.map(lambda _: VMEM, out_shape),
        out_shape=out_shape,
        compiler_params=pltpu.CompilerParams(vmem_limit_bytes=24 << 20),
    )(*args)


def shards(grad_out, routes, slots, gates, w_down, saved_gate, saved_up):
    shape = jax.ShapeDtypeStruct
    groups, shard_count, parts = (lax.axis_size(a) for a in ("group", "y", "xc"))
    capacity, lane_count = saved_gate.shape[1:]
    group = lax.axis_index("group").astype(jnp.int32)
    shard = lax.axis_index("y").astype(jnp.int32)
    column = shape((capacity, lane_count), F32)

    send = call(
        dispatch_kernel,
        [VMEM] * 4,
        shape((groups * parts, SLOTS, lane_count), BF16),
        grad_out.T,
        routes.T,
        slots.T,
        gates.T,
    )
    send, gate_pre, up_pre = lax.optimization_barrier((send, saved_gate[0], saved_up[0]))
    expert_rows = lax.all_to_all(send, ("group", "xc"), 0, 0, tiled=True)

    hidden = call(hidden_kernel, [VMEM] * 2, column, gate_pre, up_pre)
    same = lax.all_gather(
        hidden, "y", axis_index_groups=[list(range(p, shard_count, 2)) for p in (0, 1)]
    )
    other = lax.ppermute(same, "y", [(i, i ^ 1) for i in range(shard_count)])
    give, k0, k1, k2, k3, terms, gate_rows = call(
        matmul_kernel,
        [SMEM] + [VMEM] * 4,
        (
            shape((shard_count // 2, capacity, lane_count), F32),
            *[column] * 4,
            shape((groups, 1, lane_count), F32),
            column,
        ),
        jnp.stack([group, shard]),
        expert_rows.reshape(groups, parts, SLOTS, lane_count),
        w_down[0],
        same,
        other,
    )

    got = lax.ppermute(give, "y", [(i, i ^ 1) for i in range(shard_count)])
    home = lax.all_to_all(terms, "group", 0, 0, tiled=True)
    sums = [k + got[d] for d, k in enumerate((k0, k1, k2, k3))]
    for d in (2, 1, 3):
        sums[d] = lax.ppermute(
            sums[d], "y", [(i, (i + 2 * d) % shard_count) for i in range(shard_count)]
        )
    spread = call(
        spread_kernel, [VMEM], shape((shard_count * parts, 2, lane_count), F32), home
    )
    every_term = lax.all_to_all(spread, ("y", "xc"), 0, 0, tiled=True)
    out = shape((capacity, lane_count), BF16)
    grad_gate, grad_up = call(
        output_kernel, [VMEM] * 7, (out, out), *sums, gate_rows, saved_gate[0], saved_up[0]
    )
    grad_gates = call(
        collect_kernel,
        [VMEM] * 3,
        shape(routes.shape[::-1], F32),
        every_term.reshape(shard_count, parts, 2, lane_count),
        routes.T,
        slots.T,
    )
    return (grad_gate[None], grad_up[None], grad_gates.T)


def solution(mesh):
    fine = Mesh(mesh.devices.reshape(mesh.shape["group"], -1, EXP_GRP), ("group", "y", "xc"))
    local, device = ("y", "xc"), ("group", "y", "xc")
    return jax.shard_map(
        shards,
        mesh=fine,
        in_specs=(
            P("group", local),
            P("group", None),
            P("group", None),
            P("group", None),
            P(device, None, None),
            P(device, None, None),
            P(device, None, None),
        ),
        out_specs=(P(device, None, None), P(device, None, None), P("group", None)),
        check_vma=False,
    )
```

```python
import jax
import jax.numpy as jnp
from jax import lax
from jax.experimental import pallas as pl
from jax.experimental.pallas import tpu as pltpu
from jax.sharding import Mesh, PartitionSpec as P

EXP_GRP = 8
SLOTS = 16
NT = (((1,), (1,)), ((), ()))
F32 = jnp.float32
BF16 = jnp.bfloat16


def lanes(shape):
    return lax.broadcasted_iota(jnp.int32, shape, len(shape) - 1)


def rows(shape):
    return lax.broadcasted_iota(jnp.int32, shape, 0)


def dispatch_kernel(tokens_ref, routes_ref, slots_ref, gates_ref, out_ref):
    col_width, tok_count = tokens_ref.shape
    lane_count = out_ref.shape[2]
    place = routes_ref[...] * SLOTS + slots_ref[...]
    gates = gates_ref[...].astype(F32)
    spare = (lane_count - col_width, tok_count)
    features = jnp.concatenate([tokens_ref[...], jnp.zeros(spare, BF16)], axis=0)
    marks = jnp.where(rows((lane_count, tok_count)) == col_width, 1.0, 0.0).astype(BF16)
    source = jnp.concatenate([features, marks], axis=1)
    chunk = 256
    for start in range(0, out_ref.shape[0] * SLOTS, chunk):
        row_ids = rows((chunk, tok_count)) + start
        pick = jnp.zeros((chunk, tok_count), F32)
        gate = jnp.zeros((chunk, tok_count), F32)
        for k in range(place.shape[0]):
            hit = row_ids == place[k : k + 1, :]
            pick = jnp.where(hit, 1.0, pick)
            gate = jnp.where(hit, gates[k : k + 1, :], gate)
        both = jnp.concatenate([pick.astype(BF16), gate.astype(BF16)], axis=1)
        block = lax.dot_general(both, source, NT, preferred_element_type=F32)
        out_ref[start // SLOTS : (start + chunk) // SLOTS] = block.astype(BF16).reshape(
            chunk // SLOTS, SLOTS, lane_count
        )


def hidden_kernel(gate_ref, up_ref, out_ref):
    gate_pre = gate_ref[...].astype(F32)
    out_ref[...] = gate_pre * jax.nn.sigmoid(gate_pre) * up_ref[...].astype(F32)


def matmul_kernel(where_ref, rows_in, w_in, same_in, other_in, *refs):
    right_out, left_out, keep_out, gate_out, term_ref = refs[:5]
    rows_ref, w_ref, same_ref, other_ref, part_ref, gate_ref, in_sems, out_sems = refs[5:]
    groups, parts, _, lane_count = rows_ref.shape
    capacity = groups * SLOTS
    col_width = w_ref.shape[1] // parts
    count = part_ref.shape[0]
    group, shard = where_ref[0], where_ref[1]
    half = capacity // 2
    low, high = slice(0, half), slice(half, capacity)
    every = slice(0, capacity)
    routes = (
        (1, ((every, right_out, 0),)),
        (count - 1, ((every, left_out, 0),)),
        (count - 2, ((every, right_out, capacity),)),
        (2, ((every, left_out, capacity),)),
        (4, ((high, right_out, 2 * capacity), (low, left_out, 2 * capacity))),
        (0, ((every, keep_out, 0),)),
        (count - 3, ((every, keep_out, capacity),)),
        (3, ((every, keep_out, 2 * capacity),)),
    )
    units = [(shard + offset) % count for offset, _ in routes]
    arrivals = [pltpu.make_async_copy(rows_in, rows_ref, in_sems.at[0])]
    for i, unit in enumerate(units):
        span = pl.ds(pl.multiple_of(unit * lane_count, lane_count), lane_count)
        arrivals.append(pltpu.make_async_copy(w_in.at[span], w_ref.at[span], in_sems.at[i + 1]))
    arrivals.append(pltpu.make_async_copy(same_in, same_ref, in_sems.at[count + 1]))
    arrivals.append(pltpu.make_async_copy(other_in, other_ref, in_sems.at[count + 2]))
    for copy in arrivals:
        copy.start()
    arrivals[0].wait()
    departures = []

    def leave(source, target):
        departures.append(pltpu.make_async_copy(source, target, out_sems.at[len(departures)]))
        departures[-1].start()

    blocks = [rows_ref[:, e].reshape(capacity, lane_count) for e in range(parts)]
    x = jnp.concatenate([b[:, :col_width] for b in blocks], axis=1)
    row_ids, lane_ids = rows((capacity, lane_count)), lanes((capacity, lane_count))
    gate = jnp.where(lane_ids == col_width, blocks[0].astype(F32), 0.0)
    gate_ref[...] = jnp.broadcast_to(
        jnp.sum(gate, axis=1, keepdims=True), (capacity, lane_count)
    )
    leave(gate_ref, gate_out)
    for i, (_, targets) in enumerate(routes):
        arrivals[i + 1].wait()
        span = pl.ds(pl.multiple_of(units[i] * lane_count, lane_count), lane_count)
        part_ref[i] = lax.dot_general(x, w_ref[span, :], NT, preferred_element_type=F32)
        for span, out, first in targets:
            size = span.stop - span.start
            leave(part_ref.at[i, span], out.at[first : first + size])
    for copy in arrivals[count + 1 :]:
        copy.wait()
    terms = jnp.zeros((capacity, lane_count), F32)
    for i, (offset, _) in enumerate(routes):
        hidden_ref = other_ref if offset % 2 else same_ref
        terms += part_ref[i] * hidden_ref[units[i] // 2]
    total = jnp.sum(terms, axis=1, keepdims=True)
    hit = lane_ids == group % (lane_count // SLOTS) * SLOTS + row_ids % SLOTS
    term_ref[...] = jnp.sum(
        jnp.where(hit, total, 0.0).reshape(groups, SLOTS, lane_count), axis=1, keepdims=True
    )
    for copy in departures:
        copy.wait()


def middle_kernel(left_ref, right_ref, keep_ref, down_ref, up_ref):
    capacity = down_ref.shape[0]
    half = capacity // 2
    near = slice(capacity, 2 * capacity)
    down_ref[...] = keep_ref[near] + left_ref[near]
    down_ref[:half] += right_ref[2 * capacity :]
    up_ref[...] = keep_ref[2 * capacity :] + right_ref[near]
    up_ref[half:] += left_ref[2 * capacity :]


def spread_kernel(home_ref, out_ref):
    groups, _, lane_count = home_ref.shape
    half = groups // 2
    home = jnp.sum(home_ref[...].reshape(2, half, lane_count), axis=1)
    out_ref[...] = jnp.broadcast_to(home[None], out_ref.shape)


def output_kernel(
    left_ref, right_ref, keep_ref, down_ref, up_ref, gate_ref, gate_pre_ref, up_pre_ref, *outs
):
    grad_gate_ref, grad_up_ref = outs
    hidden_grad = keep_ref[...] + left_ref[...] + right_ref[...] + down_ref[...] + up_ref[...]
    gate_pre = gate_pre_ref[...].astype(F32)
    up_pre = up_pre_ref[...].astype(F32)
    sigmoid_gate = jax.nn.sigmoid(gate_pre)
    scaled = gate_ref[...] * hidden_grad
    grad_up_ref[...] = (scaled * gate_pre * sigmoid_gate).astype(BF16)
    grad_gate_ref[...] = (
        scaled * up_pre * sigmoid_gate * (1.0 + gate_pre * (1.0 - sigmoid_gate))
    ).astype(BF16)


def collect_kernel(terms_ref, routes_ref, slots_ref, out_ref):
    shard_count, experts, halves, lane_count = terms_ref.shape
    route_count, tok_count = routes_ref.shape
    table = terms_ref[0]
    for s in range(1, shard_count):
        table += terms_ref[s]
    routes = routes_ref[...]
    place = routes // EXP_GRP * SLOTS + slots_ref[...]
    for k in range(route_count):
        picked = jnp.zeros((experts, tok_count), F32)
        for h in range(halves):
            hit = rows((lane_count, tok_count)) + h * lane_count == place[k : k + 1, :]
            picked += jnp.dot(
                table[:, h, :],
                jnp.where(hit, 1.0, 0.0),
                preferred_element_type=F32,
                precision=lax.Precision.HIGHEST,
            )
        own = rows((experts, tok_count)) == routes[k : k + 1, :] % EXP_GRP
        out_ref[k : k + 1, :] = jnp.sum(jnp.where(own, picked, 0.0), axis=0, keepdims=True)


VMEM = pl.BlockSpec(memory_space=pltpu.VMEM)
SMEM = pl.BlockSpec(memory_space=pltpu.SMEM)
HBM = pl.BlockSpec(memory_space=pltpu.HBM)


def call(kernel, specs, out_shape, *args, limit=24 << 20):
    return pl.pallas_call(
        kernel,
        in_specs=specs,
        out_specs=jax.tree.map(lambda _: VMEM, out_shape),
        out_shape=out_shape,
        compiler_params=pltpu.CompilerParams(vmem_limit_bytes=limit),
    )(*args)


def shards(grad_out, routes, slots, gates, w_down, saved_gate, saved_up):
    shape = jax.ShapeDtypeStruct
    groups, shard_count, parts = (lax.axis_size(a) for a in ("group", "y", "xc"))
    capacity, lane_count = saved_gate.shape[1:]
    group = lax.axis_index("group").astype(jnp.int32)
    shard = lax.axis_index("y").astype(jnp.int32)
    column = shape((capacity, lane_count), F32)

    send = call(
        dispatch_kernel,
        [VMEM] * 4,
        shape((groups * parts, SLOTS, lane_count), BF16),
        grad_out.T,
        routes.T,
        slots.T,
        gates.T,
        limit=56 << 20,
    )
    send, gate_pre, up_pre = lax.optimization_barrier((send, saved_gate[0], saved_up[0]))
    expert_rows = lax.all_to_all(send, ("group", "xc"), 0, 0, tiled=True)

    hidden = call(hidden_kernel, [VMEM] * 2, column, gate_pre, up_pre)
    same = lax.all_gather(
        hidden, "y", axis_index_groups=[list(range(p, shard_count, 2)) for p in (0, 1)]
    )
    other = lax.ppermute(same, "y", [(i, i ^ 1) for i in range(shard_count)])
    send = shape((2 * capacity + capacity // 2, lane_count), F32)
    held = (shard_count // 2, capacity, lane_count)
    right, left, keep, gate_rows, terms = pl.pallas_call(
        matmul_kernel,
        in_specs=[SMEM] + [HBM] * 4,
        out_specs=[HBM] * 4 + [VMEM],
        out_shape=[
            send,
            send,
            shape((3 * capacity, lane_count), F32),
            column,
            shape((groups, 1, lane_count), F32),
        ],
        scratch_shapes=[
            pltpu.VMEM((groups, parts, SLOTS, lane_count), BF16),
            pltpu.VMEM(w_down.shape[1:], BF16),
            pltpu.VMEM(held, F32),
            pltpu.VMEM(held, F32),
            pltpu.VMEM((shard_count, capacity, lane_count), F32),
            pltpu.VMEM(column.shape, F32),
            pltpu.SemaphoreType.DMA((shard_count + 3,)),
            pltpu.SemaphoreType.DMA((shard_count + 2,)),
        ],
        compiler_params=pltpu.CompilerParams(vmem_limit_bytes=56 << 20),
    )(
        jnp.stack([group, shard]),
        expert_rows.reshape(groups, parts, SLOTS, lane_count),
        w_down[0],
        same,
        other,
    )

    def moved(array, by):
        return lax.ppermute(
            array, "y", [(i, (i + by) % shard_count) for i in range(shard_count)]
        )

    home = lax.all_to_all(terms, "group", 0, 0, tiled=True)
    from_left, from_right = moved(right, 1), moved(left, -1)
    down, up = call(
        middle_kernel, [VMEM] * 3, (column, column), from_left, from_right, keep
    )
    from_above, from_below = moved(down, -3), moved(up, 3)
    spread = call(
        spread_kernel, [VMEM], shape((shard_count * parts, 2, lane_count), F32), home
    )
    every_term = lax.all_to_all(spread, ("y", "xc"), 0, 0, tiled=True)
    out = shape((capacity, lane_count), BF16)
    block = pl.BlockSpec((capacity, lane_count), lambda i: (0, 0))
    grad_gate, grad_up = pl.pallas_call(
        output_kernel,
        grid=(1,),
        in_specs=[block] * 8,
        out_specs=[block] * 2,
        out_shape=[out, out],
    )(from_left, from_right, keep, from_above, from_below, gate_rows, saved_gate[0], saved_up[0])
    grad_gates = call(
        collect_kernel,
        [VMEM] * 3,
        shape(routes.shape[::-1], F32),
        every_term.reshape(shard_count, parts, 2, lane_count),
        routes.T,
        slots.T,
    )
    return (grad_gate[None], grad_up[None], grad_gates.T)


def solution(mesh):
    fine = Mesh(mesh.devices.reshape(mesh.shape["group"], -1, EXP_GRP), ("group", "y", "xc"))
    local, device = ("y", "xc"), ("group", "y", "xc")
    return jax.shard_map(
        shards,
        mesh=fine,
        in_specs=(
            P("group", local),
            P("group", None),
            P("group", None),
            P("group", None),
            P(device, None, None),
            P(device, None, None),
            P(device, None, None),
        ),
        out_specs=(P(device, None, None), P(device, None, None), P("group", None)),
        check_vma=False,
    )
```

```python
import jax
import jax.numpy as jnp
from jax import lax
from jax.experimental import pallas as pl
from jax.experimental.pallas import tpu as pltpu
from jax.sharding import Mesh, PartitionSpec as P

EXP_GRP = 8
SLOTS = 16
NT = (((1,), (1,)), ((), ()))
TN = (((0,), (0,)), ((), ()))
F32 = jnp.float32
BF16 = jnp.bfloat16


def lanes(shape):
    return lax.broadcasted_iota(jnp.int32, shape, len(shape) - 1)


def rows(shape):
    return lax.broadcasted_iota(jnp.int32, shape, 0)


def dispatch_kernel(tokens_ref, routes_ref, slots_ref, gates_ref, out_ref):
    col_width, tok_count = tokens_ref.shape
    lane_count = out_ref.shape[2]
    place = routes_ref[...] * SLOTS + slots_ref[...]
    gates = gates_ref[...].astype(F32)
    spare = (lane_count - col_width, tok_count)
    features = jnp.concatenate([tokens_ref[...], jnp.zeros(spare, BF16)], axis=0)
    marks = jnp.where(rows((lane_count, tok_count)) == col_width, 1.0, 0.0).astype(BF16)
    source = jnp.concatenate([features, marks], axis=1)
    chunk = 256
    for start in range(0, out_ref.shape[0] * SLOTS, chunk):
        row_ids = rows((chunk, tok_count)) + start
        pick = jnp.zeros((chunk, tok_count), F32)
        gate = jnp.zeros((chunk, tok_count), F32)
        for k in range(place.shape[0]):
            hit = row_ids == place[k : k + 1, :]
            pick = jnp.where(hit, 1.0, pick)
            gate = jnp.where(hit, gates[k : k + 1, :], gate)
        both = jnp.concatenate([pick.astype(BF16), gate.astype(BF16)], axis=1)
        block = lax.dot_general(both, source, NT, preferred_element_type=F32)
        out_ref[start // SLOTS : (start + chunk) // SLOTS] = block.astype(BF16).reshape(
            chunk // SLOTS, SLOTS, lane_count
        )


def hidden_kernel(gate_ref, up_ref, out_ref):
    gate_pre = gate_ref[...].astype(F32)
    out_ref[...] = gate_pre * jax.nn.sigmoid(gate_pre) * up_ref[...].astype(F32)


def matmul_kernel(shard_ref, rows_ref, w_ref, same_ref, other_ref, *outs):
    right_ref, left_ref, keep_ref, gate_ref, term_ref = outs
    groups, parts, _, lane_count = rows_ref.shape
    capacity = groups * SLOTS
    col_width = w_ref.shape[1] // parts
    count = w_ref.shape[0] // lane_count
    shard = shard_ref[0]
    half = capacity // 2
    low, high = slice(0, half), slice(half, capacity)
    every, near = slice(0, capacity), slice(capacity, 2 * capacity)
    last, spare = slice(2 * capacity, 3 * capacity), slice(2 * capacity, 2 * capacity + half)
    pairs = (
        ((1, ((every, right_ref, every),)), (count - 1, ((every, left_ref, every),))),
        ((count - 2, ((every, right_ref, near),)), (2, ((every, left_ref, near),))),
        (
            (4, ((high, right_ref, spare), (low, left_ref, spare))),
            (0, ((every, keep_ref, every),)),
        ),
        ((count - 3, ((every, keep_ref, near),)), (3, ((every, keep_ref, last),))),
    )
    blocks = [rows_ref[:, e].reshape(capacity, lane_count) for e in range(parts)]
    x = jnp.concatenate([b[:, :col_width] for b in blocks], axis=1)
    terms = jnp.zeros((capacity, lane_count), F32)
    for pair in pairs:
        units = [(shard + offset) % count for offset, _ in pair]
        firsts = [pl.multiple_of(unit * lane_count, lane_count) for unit in units]
        w = jnp.concatenate([w_ref[pl.ds(first, lane_count), :] for first in firsts], axis=0)
        both = lax.dot_general(x, w, NT, preferred_element_type=F32)
        for i, (offset, targets) in enumerate(pair):
            part = both[:, i * lane_count : (i + 1) * lane_count]
            for span, target_ref, to in targets:
                target_ref[to] = part[span]
            terms += part * (other_ref if offset % 2 else same_ref)[units[i] // 2]
    total = jnp.sum(terms, axis=1, keepdims=True)
    row_ids, lane_ids = rows((capacity, lane_count)), lanes((capacity, lane_count))
    hit = lane_ids == row_ids % lane_count
    line = jnp.sum(
        jnp.where(hit, total, 0.0).reshape(capacity // lane_count, lane_count, lane_count), axis=1
    )
    term_ref[...] = jnp.broadcast_to(line[None], term_ref.shape)
    gate = jnp.where(lane_ids == col_width, blocks[0].astype(F32), 0.0)
    gate_ref[...] = jnp.broadcast_to(
        jnp.sum(gate, axis=1, keepdims=True), (capacity, lane_count)
    )


def middle_kernel(left_ref, right_ref, keep_ref, own_ref, down_ref, up_ref):
    capacity = down_ref.shape[0]
    half = capacity // 2
    near = slice(capacity, 2 * capacity)
    own_ref[...] = keep_ref[:capacity] + left_ref[:capacity] + right_ref[:capacity]
    down_ref[...] = keep_ref[near] + left_ref[near]
    down_ref[:half] += right_ref[2 * capacity :]
    up_ref[...] = keep_ref[2 * capacity :] + right_ref[near]
    up_ref[half:] += left_ref[2 * capacity :]


def spread_kernel(terms_ref, out_ref):
    total = terms_ref[0]
    for s in range(1, terms_ref.shape[0]):
        total += terms_ref[s]
    half = out_ref.shape[0] // 2
    for h in range(2):
        out_ref[h * half : (h + 1) * half] = jnp.broadcast_to(
            total[:, h, :][None], (half, *out_ref.shape[1:])
        )


def output_kernel(own_ref, down_ref, up_ref, gate_ref, gate_pre_ref, up_pre_ref, *outs):
    grad_gate_ref, grad_up_ref = outs
    hidden_grad = own_ref[...] + down_ref[...] + up_ref[...]
    gate_pre = gate_pre_ref[...].astype(F32)
    up_pre = up_pre_ref[...].astype(F32)
    sigmoid_gate = jax.nn.sigmoid(gate_pre)
    scaled = gate_ref[...] * hidden_grad
    grad_up_ref[...] = (scaled * gate_pre * sigmoid_gate).astype(BF16)
    grad_gate_ref[...] = (
        scaled * up_pre * sigmoid_gate * (1.0 + gate_pre * (1.0 - sigmoid_gate))
    ).astype(BF16)


def collect_kernel(group_ref, terms_ref, routes_ref, slots_ref, out_ref):
    groups, parts, lane_count = terms_ref.shape
    route_count, tok_count = routes_ref.shape
    table = terms_ref[...].reshape(groups * parts, lane_count)
    offset = group_ref[0] % (lane_count // SLOTS) * SLOTS
    for k in range(route_count):
        hit = rows((groups * parts, tok_count)) == routes_ref[k : k + 1, :]
        picked = lax.dot_general(
            table,
            jnp.where(hit, 1.0, 0.0),
            TN,
            preferred_element_type=F32,
            precision=lax.Precision.HIGHEST,
        )
        own = rows((lane_count, tok_count)) == slots_ref[k : k + 1, :] + offset
        out_ref[k : k + 1, :] = jnp.sum(jnp.where(own, picked, 0.0), axis=0, keepdims=True)


VMEM = pl.BlockSpec(memory_space=pltpu.VMEM)
SMEM = pl.BlockSpec(memory_space=pltpu.SMEM)


def call(kernel, specs, out_shape, *args, limit=24 << 20):
    return pl.pallas_call(
        kernel,
        in_specs=specs,
        out_specs=jax.tree.map(lambda _: VMEM, out_shape),
        out_shape=out_shape,
        compiler_params=pltpu.CompilerParams(vmem_limit_bytes=limit),
    )(*args)


def shards(grad_out, routes, slots, gates, w_down, saved_gate, saved_up):
    shape = jax.ShapeDtypeStruct
    groups, shard_count, parts = (lax.axis_size(a) for a in ("group", "y", "xc"))
    capacity, lane_count = saved_gate.shape[1:]
    group = lax.axis_index("group").astype(jnp.int32)
    shard = lax.axis_index("y").astype(jnp.int32)
    column = shape((capacity, lane_count), F32)

    send = call(
        dispatch_kernel,
        [VMEM] * 4,
        shape((groups * parts, SLOTS, lane_count), BF16),
        grad_out.T,
        routes.T,
        slots.T,
        gates.T,
        limit=56 << 20,
    )
    send, gate_pre, up_pre = lax.optimization_barrier((send, saved_gate[0], saved_up[0]))
    expert_rows = lax.all_to_all(send, ("group", "xc"), 0, 0, tiled=True)

    hidden = call(hidden_kernel, [VMEM] * 2, column, gate_pre, up_pre)
    same = lax.all_gather(
        hidden, "y", axis_index_groups=[list(range(p, shard_count, 2)) for p in (0, 1)]
    )
    other = lax.ppermute(same, "y", [(i, i ^ 1) for i in range(shard_count)])
    send = shape((2 * capacity + capacity // 2, lane_count), F32)
    right, left, keep, gate_rows, terms = call(
        matmul_kernel,
        [SMEM] + [VMEM] * 4,
        (
            send,
            send,
            shape((3 * capacity, lane_count), F32),
            column,
            shape((shard_count * parts, 2, lane_count), F32),
        ),
        shard[None],
        expert_rows.reshape(groups, parts, SLOTS, lane_count),
        w_down[0],
        same,
        other,
        limit=56 << 20,
    )

    def moved(array, by):
        return lax.ppermute(
            array, "y", [(i, (i + by) % shard_count) for i in range(shard_count)]
        )

    every_term = lax.all_to_all(terms, ("y", "xc"), 0, 0, tiled=True)
    from_left, from_right = moved(right, 1), moved(left, -1)
    own, down, up = call(
        middle_kernel, [VMEM] * 3, (column,) * 3, from_left, from_right, keep
    )
    from_above, from_below = moved(down, -3), moved(up, 3)
    spread = call(
        spread_kernel,
        [VMEM],
        shape((groups, parts, lane_count), F32),
        every_term.reshape(shard_count, parts, 2, lane_count),
    )
    home_terms = lax.all_to_all(spread, "group", 0, 0, tiled=True)
    column_out = shape((capacity, lane_count), BF16)
    grad_gate, grad_up = call(
        output_kernel,
        [VMEM] * 6,
        (column_out, column_out),
        own,
        from_above,
        from_below,
        gate_rows,
        saved_gate[0],
        saved_up[0],
    )
    grad_gates = call(
        collect_kernel,
        [SMEM] + [VMEM] * 3,
        shape(routes.shape[::-1], F32),
        group[None],
        home_terms,
        routes.T,
        slots.T,
    )
    return (grad_gate[None], grad_up[None], grad_gates.T)


def solution(mesh):
    fine = Mesh(mesh.devices.reshape(mesh.shape["group"], -1, EXP_GRP), ("group", "y", "xc"))
    local, device = ("y", "xc"), ("group", "y", "xc")
    return jax.shard_map(
        shards,
        mesh=fine,
        in_specs=(
            P("group", local),
            P("group", None),
            P("group", None),
            P("group", None),
            P(device, None, None),
            P(device, None, None),
            P(device, None, None),
        ),
        out_specs=(P(device, None, None), P(device, None, None), P("group", None)),
        check_vma=False,
    )
```

```python
import jax
import jax.numpy as jnp
from jax import lax
from jax.experimental import pallas as pl
from jax.experimental.pallas import tpu as pltpu
from jax.sharding import Mesh, PartitionSpec as P

EXP_GRP = 8
SLOTS = 16
NT = (((1,), (1,)), ((), ()))
F32 = jnp.float32
LARGE = 56 << 20
BF16 = jnp.bfloat16


def lanes(shape):
    return lax.broadcasted_iota(jnp.int32, shape, len(shape) - 1)


def rows(shape):
    return lax.broadcasted_iota(jnp.int32, shape, 0)


def dispatch_kernel(tokens_ref, routes_ref, slots_ref, gates_ref, out_ref):
    col_width, tok_count = tokens_ref.shape
    lane_count = out_ref.shape[2]
    place = routes_ref[...] * SLOTS + slots_ref[...]
    gates = gates_ref[...].astype(F32)
    spare = (lane_count - col_width, tok_count)
    features = jnp.concatenate([tokens_ref[...], jnp.zeros(spare, BF16)], axis=0)
    marks = jnp.where(rows((lane_count, tok_count)) == col_width, 1.0, 0.0).astype(BF16)
    source = jnp.concatenate([features, marks], axis=1)
    chunk = 256
    for start in range(0, out_ref.shape[0] * SLOTS, chunk):
        row_ids = rows((chunk, tok_count)) + start
        pick = jnp.zeros((chunk, tok_count), F32)
        gate = jnp.zeros((chunk, tok_count), F32)
        for k in range(place.shape[0]):
            hit = row_ids == place[k : k + 1, :]
            pick = jnp.where(hit, 1.0, pick)
            gate = jnp.where(hit, gates[k : k + 1, :], gate)
        both = jnp.concatenate([pick.astype(BF16), gate.astype(BF16)], axis=1)
        block = lax.dot_general(both, source, NT, preferred_element_type=F32)
        out_ref[start // SLOTS : (start + chunk) // SLOTS] = block.astype(BF16).reshape(
            chunk // SLOTS, SLOTS, lane_count
        )


def hidden_kernel(gate_ref, up_ref, out_ref):
    gate_pre = gate_ref[...].astype(F32)
    out_ref[...] = gate_pre * jax.nn.sigmoid(gate_pre) * up_ref[...].astype(F32)


def matmul_kernel(where_ref, rows_ref, w_ref, same_ref, other_ref, *outs):
    give_ref, keep_ref, gate_ref, term_ref = outs
    groups, parts, _, lane_count = rows_ref.shape
    capacity = groups * SLOTS
    col_width = w_ref.shape[1] // parts
    group, shard = where_ref[0], where_ref[1]
    own, quad = shard % 2, shard // 2
    quads = give_ref.shape[0]
    blocks = [rows_ref[:, e].reshape(capacity, lane_count) for e in range(parts)]
    x = jnp.concatenate([b[:, :col_width] for b in blocks], axis=1)
    terms = jnp.zeros((capacity, lane_count), F32)
    for d in range(quads):
        target = (quad + d) % quads
        firsts = [
            pl.multiple_of((target * 2 + parity) * lane_count, lane_count)
            for parity in (1 - own, own)
        ]
        w = jnp.concatenate([w_ref[pl.ds(first, lane_count), :] for first in firsts], axis=0)
        both = lax.dot_general(x, w, NT, preferred_element_type=F32)
        give, keep = both[:, :lane_count], both[:, lane_count:]
        give_ref[d] = give
        keep_ref[d] = keep
        terms += give * other_ref[target] + keep * same_ref[target]
    total = jnp.sum(terms, axis=1, keepdims=True)
    row_ids, lane_ids = rows((capacity, lane_count)), lanes((capacity, lane_count))
    hit = lane_ids == group % (lane_count // SLOTS) * SLOTS + row_ids % SLOTS
    term_ref[...] = jnp.sum(
        jnp.where(hit, total, 0.0).reshape(groups, SLOTS, lane_count), axis=1, keepdims=True
    )
    gate = jnp.where(lane_ids == col_width, blocks[0].astype(F32), 0.0)
    gate_ref[...] = jnp.broadcast_to(
        jnp.sum(gate, axis=1, keepdims=True), (capacity, lane_count)
    )


def spread_kernel(home_ref, out_ref):
    groups, _, lane_count = home_ref.shape
    half = groups // 2
    home = jnp.sum(home_ref[...].reshape(2, half, lane_count), axis=1)
    out_ref[...] = jnp.broadcast_to(home[None], out_ref.shape)


def output_kernel(h0, h1, h2, h3, gate_ref, gate_pre_ref, up_pre_ref, grad_gate_ref, grad_up_ref):
    hidden_grad = h0[...] + h1[...] + h2[...] + h3[...]
    gate_pre = gate_pre_ref[...].astype(F32)
    up_pre = up_pre_ref[...].astype(F32)
    sigmoid_gate = jax.nn.sigmoid(gate_pre)
    scaled = gate_ref[...] * hidden_grad
    grad_up_ref[...] = (scaled * gate_pre * sigmoid_gate).astype(BF16)
    grad_gate_ref[...] = (
        scaled * up_pre * sigmoid_gate * (1.0 + gate_pre * (1.0 - sigmoid_gate))
    ).astype(BF16)


def collect_kernel(terms_ref, routes_ref, slots_ref, out_ref):
    shard_count, experts, halves, lane_count = terms_ref.shape
    route_count, tok_count = routes_ref.shape
    table = terms_ref[0]
    for s in range(1, shard_count):
        table += terms_ref[s]
    routes = routes_ref[...]
    place = routes // EXP_GRP * SLOTS + slots_ref[...]
    for k in range(route_count):
        picked = jnp.zeros((experts, tok_count), F32)
        for h in range(halves):
            hit = rows((lane_count, tok_count)) + h * lane_count == place[k : k + 1, :]
            picked += jnp.dot(
                table[:, h, :],
                jnp.where(hit, 1.0, 0.0),
                preferred_element_type=F32,
                precision=lax.Precision.HIGHEST,
            )
        own = rows((experts, tok_count)) == routes[k : k + 1, :] % EXP_GRP
        out_ref[k : k + 1, :] = jnp.sum(jnp.where(own, picked, 0.0), axis=0, keepdims=True)


VMEM = pl.BlockSpec(memory_space=pltpu.VMEM)
SMEM = pl.BlockSpec(memory_space=pltpu.SMEM)


def call(kernel, specs, out_shape, *args, limit=24 << 20):
    return pl.pallas_call(
        kernel,
        in_specs=specs,
        out_specs=jax.tree.map(lambda _: VMEM, out_shape),
        out_shape=out_shape,
        compiler_params=pltpu.CompilerParams(vmem_limit_bytes=limit),
    )(*args)


def shards(grad_out, routes, slots, gates, w_down, saved_gate, saved_up):
    shape = jax.ShapeDtypeStruct
    groups, shard_count, parts = (lax.axis_size(a) for a in ("group", "y", "xc"))
    capacity, lane_count = saved_gate.shape[1:]
    group = lax.axis_index("group").astype(jnp.int32)
    shard = lax.axis_index("y").astype(jnp.int32)
    column = shape((capacity, lane_count), F32)

    send = call(
        dispatch_kernel,
        [VMEM] * 4,
        shape((groups * parts, SLOTS, lane_count), BF16),
        grad_out.T,
        routes.T,
        slots.T,
        gates.T,
        limit=LARGE,
    )
    send, gate_pre, up_pre = lax.optimization_barrier((send, saved_gate[0], saved_up[0]))
    expert_rows = lax.all_to_all(send, ("group", "xc"), 0, 0, tiled=True)

    hidden = call(hidden_kernel, [VMEM] * 2, column, gate_pre, up_pre, limit=LARGE)
    same = lax.all_gather(
        hidden, "y", axis_index_groups=[list(range(p, shard_count, 2)) for p in (0, 1)]
    )
    quads = shard_count // 2
    other = lax.ppermute(same, "y", [(i, i ^ 1) for i in range(shard_count)])
    give, keep, gate_rows, terms = call(
        matmul_kernel,
        [SMEM] + [VMEM] * 4,
        (
            shape((quads, capacity, lane_count), F32),
            shape((quads, capacity, lane_count), F32),
            column,
            shape((groups, 1, lane_count), F32),
        ),
        jnp.stack([group, shard]),
        expert_rows.reshape(groups, parts, SLOTS, lane_count),
        w_down[0],
        same,
        other,
        limit=LARGE,
    )

    got = lax.ppermute(give, "y", [(i, i ^ 1) for i in range(shard_count)])
    home = lax.all_to_all(terms, "group", 0, 0, tiled=True)
    sums = [keep[d] + got[d] for d in range(quads)]
    for d in (2, 1, 3):
        sums[d] = lax.ppermute(
            sums[d], "y", [(i, (i + 2 * d) % shard_count) for i in range(shard_count)]
        )
    spread = call(
        spread_kernel, [VMEM], shape((shard_count * parts, 2, lane_count), F32), home
    )
    every_term = lax.all_to_all(spread, ("y", "xc"), 0, 0, tiled=True)
    out = shape((capacity, lane_count), BF16)
    grad_gate, grad_up = call(
        output_kernel, [VMEM] * 7, (out, out), *sums, gate_rows, saved_gate[0], saved_up[0]
    )
    every_term, grad_gate, grad_up = lax.optimization_barrier((every_term, grad_gate, grad_up))
    grad_gates = call(
        collect_kernel,
        [VMEM] * 3,
        shape(routes.shape[::-1], F32),
        every_term.reshape(shard_count, parts, 2, lane_count),
        routes.T,
        slots.T,
    )
    return (grad_gate[None], grad_up[None], grad_gates.T)


def solution(mesh):
    fine = Mesh(mesh.devices.reshape(mesh.shape["group"], -1, EXP_GRP), ("group", "y", "xc"))
    local, device = ("y", "xc"), ("group", "y", "xc")
    return jax.shard_map(
        shards,
        mesh=fine,
        in_specs=(
            P("group", local),
            P("group", None),
            P("group", None),
            P("group", None),
            P(device, None, None),
            P(device, None, None),
            P(device, None, None),
        ),
        out_specs=(P(device, None, None), P(device, None, None), P("group", None)),
        check_vma=False,
    )
```

```python
import jax
import jax.numpy as jnp
from jax import lax
from jax.experimental import pallas as pl
from jax.experimental.pallas import tpu as pltpu
from jax.sharding import Mesh, PartitionSpec as P

EXP_GRP = 8
SLOTS = 16
NT = (((1,), (1,)), ((), ()))
F32 = jnp.float32
LARGE = 56 << 20
BF16 = jnp.bfloat16


def lanes(shape):
    return lax.broadcasted_iota(jnp.int32, shape, len(shape) - 1)


def rows(shape):
    return lax.broadcasted_iota(jnp.int32, shape, 0)


def dispatch_kernel(
    tokens_ref, routes_ref, slots_ref, gates_ref, gate_pre_ref, up_pre_ref, out_ref, hidden_ref
):
    col_width, tok_count = tokens_ref.shape
    lane_count = out_ref.shape[2]
    place = routes_ref[...] * SLOTS + slots_ref[...]
    gates = gates_ref[...].astype(F32)
    spare = (lane_count - col_width, tok_count)
    features = jnp.concatenate([tokens_ref[...], jnp.zeros(spare, BF16)], axis=0)
    marks = jnp.where(rows((lane_count, tok_count)) == col_width, 1.0, 0.0).astype(BF16)
    source = jnp.concatenate([features, marks], axis=1)
    chunk = 256
    for start in range(0, out_ref.shape[0] * SLOTS, chunk):
        row_ids = rows((chunk, tok_count)) + start
        gate = jnp.zeros((chunk, tok_count), F32)
        for k in range(place.shape[0]):
            gate = jnp.where(row_ids == place[k : k + 1, :], gates[k : k + 1, :], gate)
        pick = jnp.where(gate > 0.0, 1.0, 0.0)
        both = jnp.concatenate([pick.astype(BF16), gate.astype(BF16)], axis=1)
        block = lax.dot_general(both, source, NT, preferred_element_type=F32)
        out_ref[start // SLOTS : (start + chunk) // SLOTS] = block.astype(BF16).reshape(
            chunk // SLOTS, SLOTS, lane_count
        )
    gate_pre = gate_pre_ref[...].astype(F32)
    hidden_ref[...] = gate_pre * jax.nn.sigmoid(gate_pre) * up_pre_ref[...].astype(F32)


def matmul_kernel(shard_ref, rows_ref, w_ref, same_ref, give_ref, keep_ref, gate_ref, base_ref):
    groups, parts, _, lane_count = rows_ref.shape
    capacity = groups * SLOTS
    col_width = w_ref.shape[1] // parts
    own, quad = shard_ref[0] % 2, shard_ref[0] // 2
    quads = give_ref.shape[0]
    blocks = [rows_ref[:, e].reshape(capacity, lane_count) for e in range(parts)]
    x = jnp.concatenate([b[:, :col_width] for b in blocks], axis=1)
    terms = jnp.zeros((capacity, lane_count), F32)
    for d in range(quads):
        target = (quad + d) % quads
        firsts = [
            pl.multiple_of((target * 2 + parity) * lane_count, lane_count)
            for parity in (1 - own, own)
        ]
        w = jnp.concatenate([w_ref[pl.ds(first, lane_count), :] for first in firsts], axis=0)
        both = lax.dot_general(x, w, NT, preferred_element_type=F32)
        give_ref[d] = both[:, :lane_count]
        keep_ref[d] = both[:, lane_count:]
        terms += both[:, lane_count:] * same_ref[target]
    base_ref[...] = terms
    gate = jnp.where(lanes((capacity, lane_count)) == col_width, blocks[0].astype(F32), 0.0)
    gate_ref[...] = jnp.broadcast_to(
        jnp.sum(gate, axis=1, keepdims=True), (capacity, lane_count)
    )


def terms_kernel(group_ref, shard_ref, give_ref, other_ref, base_ref, term_ref):
    quads, capacity, lane_count = give_ref.shape
    groups = term_ref.shape[0]
    group, quad = group_ref[0], shard_ref[0] // 2
    terms = base_ref[...]
    for d in range(quads):
        terms += give_ref[d] * other_ref[(quad + d) % quads]
    total = jnp.sum(terms, axis=1, keepdims=True)
    row_ids, lane_ids = rows((capacity, lane_count)), lanes((capacity, lane_count))
    hit = lane_ids == group % (lane_count // SLOTS) * SLOTS + row_ids % SLOTS
    term_ref[...] = jnp.sum(
        jnp.where(hit, total, 0.0).reshape(groups, SLOTS, lane_count), axis=1, keepdims=True
    )


def spread_kernel(home_ref, out_ref):
    groups, _, lane_count = home_ref.shape
    half = groups // 2
    home = jnp.sum(home_ref[...].reshape(2, half, lane_count), axis=1)
    out_ref[...] = jnp.broadcast_to(home[None], out_ref.shape)


def output_kernel(h0, h1, h2, h3, gate_ref, gate_pre_ref, up_pre_ref, grad_gate_ref, grad_up_ref):
    hidden_grad = h0[...] + h1[...] + h2[...] + h3[...]
    gate_pre = gate_pre_ref[...].astype(F32)
    up_pre = up_pre_ref[...].astype(F32)
    sigmoid_gate = jax.nn.sigmoid(gate_pre)
    scaled = gate_ref[...] * hidden_grad
    grad_up_ref[...] = (scaled * gate_pre * sigmoid_gate).astype(BF16)
    grad_gate_ref[...] = (
        scaled * up_pre * sigmoid_gate * (1.0 + gate_pre * (1.0 - sigmoid_gate))
    ).astype(BF16)


def collect_kernel(terms_ref, routes_ref, slots_ref, out_ref):
    shard_count, experts, halves, lane_count = terms_ref.shape
    route_count, tok_count = routes_ref.shape
    table = terms_ref[0]
    for s in range(1, shard_count):
        table += terms_ref[s]
    routes = routes_ref[...]
    place = routes // EXP_GRP * SLOTS + slots_ref[...]
    places = jnp.concatenate([place[k : k + 1, :] for k in range(route_count)], axis=1)
    picked = jnp.zeros((experts, route_count * tok_count), F32)
    for h in range(halves):
        rest = table[:, h, :]
        parts = []
        for _ in range(3):
            part = rest.astype(BF16)
            parts.append(part)
            rest = rest - part.astype(F32)
        hit = rows((lane_count, route_count * tok_count)) + h * lane_count == places
        every = jnp.dot(
            jnp.concatenate(parts, axis=0),
            jnp.where(hit, 1.0, 0.0).astype(BF16),
            preferred_element_type=F32,
        )
        for i in range(3):
            picked += every[i * experts : (i + 1) * experts]
    for k in range(route_count):
        own = rows((experts, tok_count)) == routes[k : k + 1, :] % EXP_GRP
        column = picked[:, k * tok_count : (k + 1) * tok_count]
        out_ref[k : k + 1, :] = jnp.sum(jnp.where(own, column, 0.0), axis=0, keepdims=True)


VMEM = pl.BlockSpec(memory_space=pltpu.VMEM)
SMEM = pl.BlockSpec(memory_space=pltpu.SMEM)


def call(kernel, specs, out_shape, *args, limit=24 << 20):
    return pl.pallas_call(
        kernel,
        in_specs=specs,
        out_specs=jax.tree.map(lambda _: VMEM, out_shape),
        out_shape=out_shape,
        compiler_params=pltpu.CompilerParams(vmem_limit_bytes=limit),
    )(*args)


def shards(grad_out, routes, slots, gates, w_down, saved_gate, saved_up):
    shape = jax.ShapeDtypeStruct
    groups, shard_count, parts = (lax.axis_size(a) for a in ("group", "y", "xc"))
    capacity, lane_count = saved_gate.shape[1:]
    group = lax.axis_index("group").astype(jnp.int32)
    shard = lax.axis_index("y").astype(jnp.int32)
    column = shape((capacity, lane_count), F32)

    send, hidden = call(
        dispatch_kernel,
        [VMEM] * 6,
        (shape((groups * parts, SLOTS, lane_count), BF16), column),
        grad_out.T,
        routes.T,
        slots.T,
        gates.T,
        saved_gate[0],
        saved_up[0],
        limit=LARGE,
    )
    expert_rows = lax.all_to_all(send, ("group", "xc"), 0, 0, tiled=True)

    same = lax.all_gather(
        hidden, "y", axis_index_groups=[list(range(p, shard_count, 2)) for p in (0, 1)]
    )
    quads = shard_count // 2
    other = lax.ppermute(same, "y", [(i, i ^ 1) for i in range(shard_count)])
    held = shape((quads, capacity, lane_count), F32)
    give, keep, gate_rows, base = call(
        matmul_kernel,
        [SMEM] + [VMEM] * 3,
        (held, held, column, column),
        shard[None],
        expert_rows.reshape(groups, parts, SLOTS, lane_count),
        w_down[0],
        same,
        limit=LARGE,
    )
    terms = call(
        terms_kernel,
        [SMEM] * 2 + [VMEM] * 3,
        shape((groups, 1, lane_count), F32),
        group[None],
        shard[None],
        give,
        other,
        base,
        limit=LARGE,
    )

    got = lax.ppermute(give, "y", [(i, i ^ 1) for i in range(shard_count)])
    home = lax.all_to_all(terms, "group", 0, 0, tiled=True)
    sums = [keep[d] + got[d] for d in range(quads)]
    for d in (2, 1, 3):
        sums[d] = lax.ppermute(
            sums[d], "y", [(i, (i + 2 * d) % shard_count) for i in range(shard_count)]
        )
    spread = call(
        spread_kernel, [VMEM], shape((shard_count * parts, 2, lane_count), F32), home
    )
    every_term = lax.all_to_all(spread, ("y", "xc"), 0, 0, tiled=True)
    out = shape((capacity, lane_count), BF16)
    grad_gate, grad_up = call(
        output_kernel, [VMEM] * 7, (out, out), *sums, gate_rows, saved_gate[0], saved_up[0]
    )
    every_term, grad_gate, grad_up = lax.optimization_barrier((every_term, grad_gate, grad_up))
    grad_gates = call(
        collect_kernel,
        [VMEM] * 3,
        shape(routes.shape[::-1], F32),
        every_term.reshape(shard_count, parts, 2, lane_count),
        routes.T,
        slots.T,
    )
    return (grad_gate[None], grad_up[None], grad_gates.T)


def solution(mesh):
    fine = Mesh(mesh.devices.reshape(mesh.shape["group"], -1, EXP_GRP), ("group", "y", "xc"))
    local, device = ("y", "xc"), ("group", "y", "xc")
    return jax.shard_map(
        shards,
        mesh=fine,
        in_specs=(
            P("group", local),
            P("group", None),
            P("group", None),
            P("group", None),
            P(device, None, None),
            P(device, None, None),
            P(device, None, None),
        ),
        out_specs=(P(device, None, None), P(device, None, None), P("group", None)),
        check_vma=False,
    )
```

```python
import jax
import jax.numpy as jnp
from jax import lax
from jax.experimental import pallas as pl
from jax.experimental.pallas import tpu as pltpu
from jax.sharding import Mesh, PartitionSpec as P

EXP_GRP = 8
SLOTS = 16
NT = (((1,), (1,)), ((), ()))
F32 = jnp.float32
LARGE = 56 << 20
BF16 = jnp.bfloat16


def lanes(shape):
    return lax.broadcasted_iota(jnp.int32, shape, len(shape) - 1)


def rows(shape):
    return lax.broadcasted_iota(jnp.int32, shape, 0)


def dispatch_kernel(
    tokens_ref, routes_ref, slots_ref, gates_ref, gate_pre_ref, up_pre_ref, out_ref, hidden_ref
):
    col_width, tok_count = tokens_ref.shape
    lane_count = out_ref.shape[2]
    place = routes_ref[...] * SLOTS + slots_ref[...]
    gates = gates_ref[...].astype(F32)
    spare = (lane_count - col_width, tok_count)
    features = jnp.concatenate([tokens_ref[...], jnp.zeros(spare, BF16)], axis=0)
    marks = jnp.where(rows((lane_count, tok_count)) == col_width, 1.0, 0.0).astype(BF16)
    source = jnp.concatenate([features, marks], axis=1)
    chunk = 256
    for start in range(0, out_ref.shape[0] * SLOTS, chunk):
        row_ids = rows((chunk, tok_count)) + start
        gate = jnp.zeros((chunk, tok_count), F32)
        for k in range(place.shape[0]):
            gate = jnp.where(row_ids == place[k : k + 1, :], gates[k : k + 1, :], gate)
        pick = jnp.where(gate > 0.0, 1.0, 0.0)
        both = jnp.concatenate([pick.astype(BF16), gate.astype(BF16)], axis=1)
        block = lax.dot_general(both, source, NT, preferred_element_type=F32)
        out_ref[start // SLOTS : (start + chunk) // SLOTS] = block.astype(BF16).reshape(
            chunk // SLOTS, SLOTS, lane_count
        )
    gate_pre = gate_pre_ref[...].astype(F32)
    hidden_ref[...] = gate_pre * jax.nn.sigmoid(gate_pre) * up_pre_ref[...].astype(F32)


def matmul_kernel(
    shard_ref, rows_ref, w_ref, same_ref, right_ref, left_ref, keep_ref, gate_ref, base_ref
):
    groups, parts, _, lane_count = rows_ref.shape
    capacity = groups * SLOTS
    col_width = w_ref.shape[1] // parts
    count = w_ref.shape[0] // lane_count
    shard = shard_ref[0]
    half = capacity // 2
    low, high = slice(0, half), slice(half, capacity)
    every, near = slice(0, capacity), slice(capacity, 2 * capacity)
    last, spare = slice(2 * capacity, 3 * capacity), slice(2 * capacity, 2 * capacity + half)
    pairs = (
        ((1, ((every, right_ref, every),)), (count - 1, ((every, left_ref, every),))),
        ((count - 2, ((every, right_ref, near),)), (2, ((every, left_ref, near),))),
        (
            (4, ((high, right_ref, spare), (low, left_ref, spare))),
            (0, ((every, keep_ref, every),)),
        ),
        ((count - 3, ((every, keep_ref, near),)), (3, ((every, keep_ref, last),))),
    )
    blocks = [rows_ref[:, e].reshape(capacity, lane_count) for e in range(parts)]
    x = jnp.concatenate([b[:, :col_width] for b in blocks], axis=1)
    terms = jnp.zeros((capacity, lane_count), F32)
    for pair in pairs:
        units = [(shard + offset) % count for offset, _ in pair]
        firsts = [pl.multiple_of(unit * lane_count, lane_count) for unit in units]
        w = jnp.concatenate([w_ref[pl.ds(first, lane_count), :] for first in firsts], axis=0)
        both = lax.dot_general(x, w, NT, preferred_element_type=F32)
        for i, (offset, targets) in enumerate(pair):
            part = both[:, i * lane_count : (i + 1) * lane_count]
            for span, target_ref, to in targets:
                target_ref[to] = part[span]
            if offset % 2 == 0:
                terms += part * same_ref[units[i] // 2]
    base_ref[...] = terms
    gate = jnp.where(lanes((capacity, lane_count)) == col_width, blocks[0].astype(F32), 0.0)
    gate_ref[...] = jnp.broadcast_to(
        jnp.sum(gate, axis=1, keepdims=True), (capacity, lane_count)
    )


def terms_kernel(
    group_ref, shard_ref, right_ref, left_ref, keep_ref, other_ref, base_ref, term_ref
):
    capacity, lane_count = base_ref.shape
    groups = term_ref.shape[0]
    count = 2 * other_ref.shape[0]
    group, shard = group_ref[0], shard_ref[0]
    terms = base_ref[...]
    for offset, part_ref, first in (
        (1, right_ref, 0),
        (count - 1, left_ref, 0),
        (count - 3, keep_ref, capacity),
        (3, keep_ref, 2 * capacity),
    ):
        unit = (shard + offset) % count
        terms += part_ref[first : first + capacity] * other_ref[unit // 2]
    total = jnp.sum(terms, axis=1, keepdims=True)
    row_ids, lane_ids = rows((capacity, lane_count)), lanes((capacity, lane_count))
    hit = lane_ids == group % (lane_count // SLOTS) * SLOTS + row_ids % SLOTS
    term_ref[...] = jnp.sum(
        jnp.where(hit, total, 0.0).reshape(groups, SLOTS, lane_count), axis=1, keepdims=True
    )


def middle_kernel(left_ref, right_ref, keep_ref, own_ref, down_ref, up_ref):
    capacity = down_ref.shape[0]
    half = capacity // 2
    near = slice(capacity, 2 * capacity)
    own_ref[...] = keep_ref[:capacity] + left_ref[:capacity] + right_ref[:capacity]
    down_ref[...] = keep_ref[near] + left_ref[near]
    down_ref[:half] += right_ref[2 * capacity :]
    up_ref[...] = keep_ref[2 * capacity :] + right_ref[near]
    up_ref[half:] += left_ref[2 * capacity :]


def spread_kernel(home_ref, out_ref):
    groups, _, lane_count = home_ref.shape
    half = groups // 2
    home = jnp.sum(home_ref[...].reshape(2, half, lane_count), axis=1)
    out_ref[...] = jnp.broadcast_to(home[None], out_ref.shape)


def output_kernel(own_ref, down_ref, up_ref, gate_ref, gate_pre_ref, up_pre_ref, *outs):
    grad_gate_ref, grad_up_ref = outs
    hidden_grad = own_ref[...] + down_ref[...] + up_ref[...]
    gate_pre = gate_pre_ref[...].astype(F32)
    up_pre = up_pre_ref[...].astype(F32)
    sigmoid_gate = jax.nn.sigmoid(gate_pre)
    scaled = gate_ref[...] * hidden_grad
    grad_up_ref[...] = (scaled * gate_pre * sigmoid_gate).astype(BF16)
    grad_gate_ref[...] = (
        scaled * up_pre * sigmoid_gate * (1.0 + gate_pre * (1.0 - sigmoid_gate))
    ).astype(BF16)


def collect_kernel(terms_ref, routes_ref, slots_ref, out_ref):
    shard_count, experts, halves, lane_count = terms_ref.shape
    route_count, tok_count = routes_ref.shape
    table = terms_ref[0]
    for s in range(1, shard_count):
        table += terms_ref[s]
    routes = routes_ref[...]
    place = routes // EXP_GRP * SLOTS + slots_ref[...]
    places = jnp.concatenate([place[k : k + 1, :] for k in range(route_count)], axis=1)
    picked = jnp.zeros((experts, route_count * tok_count), F32)
    for h in range(halves):
        rest = table[:, h, :]
        parts = []
        for _ in range(3):
            part = rest.astype(BF16)
            parts.append(part)
            rest = rest - part.astype(F32)
        hit = rows((lane_count, route_count * tok_count)) + h * lane_count == places
        every = jnp.dot(
            jnp.concatenate(parts, axis=0),
            jnp.where(hit, 1.0, 0.0).astype(BF16),
            preferred_element_type=F32,
        )
        for i in range(3):
            picked += every[i * experts : (i + 1) * experts]
    for k in range(route_count):
        own = rows((experts, tok_count)) == routes[k : k + 1, :] % EXP_GRP
        column = picked[:, k * tok_count : (k + 1) * tok_count]
        out_ref[k : k + 1, :] = jnp.sum(jnp.where(own, column, 0.0), axis=0, keepdims=True)


VMEM = pl.BlockSpec(memory_space=pltpu.VMEM)
SMEM = pl.BlockSpec(memory_space=pltpu.SMEM)


def call(kernel, specs, out_shape, *args, limit=24 << 20):
    return pl.pallas_call(
        kernel,
        in_specs=specs,
        out_specs=jax.tree.map(lambda _: VMEM, out_shape),
        out_shape=out_shape,
        compiler_params=pltpu.CompilerParams(vmem_limit_bytes=limit),
    )(*args)


def shards(grad_out, routes, slots, gates, w_down, saved_gate, saved_up):
    shape = jax.ShapeDtypeStruct
    groups, shard_count, parts = (lax.axis_size(a) for a in ("group", "y", "xc"))
    capacity, lane_count = saved_gate.shape[1:]
    group = lax.axis_index("group").astype(jnp.int32)
    shard = lax.axis_index("y").astype(jnp.int32)
    column = shape((capacity, lane_count), F32)

    send, hidden = call(
        dispatch_kernel,
        [VMEM] * 6,
        (shape((groups * parts, SLOTS, lane_count), BF16), column),
        grad_out.T,
        routes.T,
        slots.T,
        gates.T,
        saved_gate[0],
        saved_up[0],
        limit=LARGE,
    )
    expert_rows = lax.all_to_all(send, ("group", "xc"), 0, 0, tiled=True)

    same = lax.all_gather(
        hidden, "y", axis_index_groups=[list(range(p, shard_count, 2)) for p in (0, 1)]
    )
    quads = shard_count // 2
    other = lax.ppermute(same, "y", [(i, i ^ 1) for i in range(shard_count)])
    send_shape = shape((2 * capacity + capacity // 2, lane_count), F32)
    right, left, keep, gate_rows, base = call(
        matmul_kernel,
        [SMEM] + [VMEM] * 3,
        (send_shape, send_shape, shape((3 * capacity, lane_count), F32), column, column),
        shard[None],
        expert_rows.reshape(groups, parts, SLOTS, lane_count),
        w_down[0],
        same,
        limit=LARGE,
    )
    terms = call(
        terms_kernel,
        [SMEM] * 2 + [VMEM] * 5,
        shape((groups, 1, lane_count), F32),
        group[None],
        shard[None],
        right,
        left,
        keep,
        other,
        base,
        limit=LARGE,
    )

    def moved(array, by):
        return lax.ppermute(
            array, "y", [(i, (i + by) % shard_count) for i in range(shard_count)]
        )

    from_left, from_right = moved(right, 1), moved(left, -1)
    home = lax.all_to_all(terms, "group", 0, 0, tiled=True)
    own, down, up = call(
        middle_kernel, [VMEM] * 3, (column,) * 3, from_left, from_right, keep
    )
    from_above, from_below = moved(down, -3), moved(up, 3)
    spread = call(
        spread_kernel, [VMEM], shape((shard_count * parts, 2, lane_count), F32), home
    )
    every_term = lax.all_to_all(spread, ("y", "xc"), 0, 0, tiled=True)
    out = shape((capacity, lane_count), BF16)
    grad_gate, grad_up = call(
        output_kernel,
        [VMEM] * 6,
        (out, out),
        own,
        from_above,
        from_below,
        gate_rows,
        saved_gate[0],
        saved_up[0],
    )
    every_term, grad_gate, grad_up = lax.optimization_barrier((every_term, grad_gate, grad_up))
    grad_gates = call(
        collect_kernel,
        [VMEM] * 3,
        shape(routes.shape[::-1], F32),
        every_term.reshape(shard_count, parts, 2, lane_count),
        routes.T,
        slots.T,
    )
    return (grad_gate[None], grad_up[None], grad_gates.T)


def solution(mesh):
    fine = Mesh(mesh.devices.reshape(mesh.shape["group"], -1, EXP_GRP), ("group", "y", "xc"))
    local, device = ("y", "xc"), ("group", "y", "xc")
    return jax.shard_map(
        shards,
        mesh=fine,
        in_specs=(
            P("group", local),
            P("group", None),
            P("group", None),
            P("group", None),
            P(device, None, None),
            P(device, None, None),
            P(device, None, None),
        ),
        out_specs=(P(device, None, None), P(device, None, None), P("group", None)),
        check_vma=False,
    )
```

```python
import jax
import jax.numpy as jnp
from jax import lax
from jax.experimental import pallas as pl
from jax.experimental.pallas import tpu as pltpu
from jax.sharding import Mesh, PartitionSpec as P

EXP_GRP = 8
SLOTS = 16
NT = (((1,), (1,)), ((), ()))
F32 = jnp.float32
LARGE = 56 << 20
BF16 = jnp.bfloat16


def lanes(shape):
    return lax.broadcasted_iota(jnp.int32, shape, len(shape) - 1)


def rows(shape):
    return lax.broadcasted_iota(jnp.int32, shape, 0)


def dispatch_kernel(
    tokens_ref, routes_ref, slots_ref, gates_ref, gate_pre_ref, up_pre_ref, out_ref, hidden_ref
):
    col_width, tok_count = tokens_ref.shape
    lane_count = out_ref.shape[2]
    place = routes_ref[...] * SLOTS + slots_ref[...]
    gates = gates_ref[...].astype(F32)
    spare = (lane_count - col_width, tok_count)
    features = jnp.concatenate([tokens_ref[...], jnp.zeros(spare, BF16)], axis=0)
    marks = jnp.where(rows((lane_count, tok_count)) == col_width, 1.0, 0.0).astype(BF16)
    source = jnp.concatenate([features, marks], axis=1)
    chunk = 256
    for start in range(0, out_ref.shape[0] * SLOTS, chunk):
        row_ids = rows((chunk, tok_count)) + start
        gate = jnp.zeros((chunk, tok_count), F32)
        for k in range(place.shape[0]):
            gate = jnp.where(row_ids == place[k : k + 1, :], gates[k : k + 1, :], gate)
        pick = jnp.where(gate > 0.0, 1.0, 0.0)
        both = jnp.concatenate([pick.astype(BF16), gate.astype(BF16)], axis=1)
        block = lax.dot_general(both, source, NT, preferred_element_type=F32)
        out_ref[start // SLOTS : (start + chunk) // SLOTS] = block.astype(BF16).reshape(
            chunk // SLOTS, SLOTS, lane_count
        )
    gate_pre = gate_pre_ref[...].astype(F32)
    hidden_ref[...] = gate_pre * jax.nn.sigmoid(gate_pre) * up_pre_ref[...].astype(F32)


def matmul_kernel(
    shard_ref, rows_ref, w_ref, same_ref, right_ref, left_ref, keep_ref, gate_ref, base_ref
):
    groups, parts, _, lane_count = rows_ref.shape
    capacity = groups * SLOTS
    col_width = w_ref.shape[1] // parts
    count = w_ref.shape[0] // lane_count
    shard = shard_ref[0]
    half = capacity // 2
    low, high = slice(0, half), slice(half, capacity)
    every, near = slice(0, capacity), slice(capacity, 2 * capacity)
    last, spare = slice(2 * capacity, 3 * capacity), slice(2 * capacity, 2 * capacity + half)
    pairs = (
        ((1, ((every, right_ref, every),)), (count - 1, ((every, left_ref, every),))),
        ((count - 2, ((every, right_ref, near),)), (2, ((every, left_ref, near),))),
        (
            (4, ((high, right_ref, spare), (low, left_ref, spare))),
            (0, ((every, keep_ref, every),)),
        ),
        ((count - 3, ((every, keep_ref, near),)), (3, ((every, keep_ref, last),))),
    )
    blocks = [rows_ref[:, e].reshape(capacity, lane_count) for e in range(parts)]
    x = jnp.concatenate([b[:, :col_width] for b in blocks], axis=1)
    terms = jnp.zeros((capacity, lane_count), F32)
    for pair in pairs:
        units = [(shard + offset) % count for offset, _ in pair]
        firsts = [pl.multiple_of(unit * lane_count, lane_count) for unit in units]
        w = jnp.concatenate([w_ref[pl.ds(first, lane_count), :] for first in firsts], axis=0)
        both = lax.dot_general(x, w, NT, preferred_element_type=F32)
        for i, (offset, targets) in enumerate(pair):
            part = both[:, i * lane_count : (i + 1) * lane_count]
            for span, target_ref, to in targets:
                target_ref[to] = part[span]
            if offset % 2 == 0:
                terms += part * same_ref[units[i] // 2]
    base_ref[...] = terms
    gate = jnp.where(lanes((capacity, lane_count)) == col_width, blocks[0].astype(F32), 0.0)
    gate_ref[...] = jnp.broadcast_to(
        jnp.sum(gate, axis=1, keepdims=True), (capacity, lane_count)
    )


def terms_kernel(
    group_ref, shard_ref, right_ref, left_ref, keep_ref, other_ref, base_ref, term_ref
):
    capacity, lane_count = base_ref.shape
    groups = term_ref.shape[0]
    count = 2 * other_ref.shape[0]
    group, shard = group_ref[0], shard_ref[0]
    terms = base_ref[...]
    for offset, part_ref, first in (
        (1, right_ref, 0),
        (count - 1, left_ref, 0),
        (count - 3, keep_ref, capacity),
        (3, keep_ref, 2 * capacity),
    ):
        unit = (shard + offset) % count
        terms += part_ref[first : first + capacity] * other_ref[unit // 2]
    total = jnp.sum(terms, axis=1, keepdims=True)
    row_ids, lane_ids = rows((capacity, lane_count)), lanes((capacity, lane_count))
    hit = lane_ids == group % (lane_count // SLOTS) * SLOTS + row_ids % SLOTS
    term_ref[...] = jnp.sum(
        jnp.where(hit, total, 0.0).reshape(groups, SLOTS, lane_count), axis=1, keepdims=True
    )


def middle_kernel(left_ref, right_ref, keep_ref, own_ref, down_ref, up_ref):
    capacity = down_ref.shape[0]
    half = capacity // 2
    near = slice(capacity, 2 * capacity)
    own_ref[...] = keep_ref[:capacity] + left_ref[:capacity] + right_ref[:capacity]
    down_ref[...] = keep_ref[near] + left_ref[near]
    down_ref[:half] += right_ref[2 * capacity :]
    up_ref[...] = keep_ref[2 * capacity :] + right_ref[near]
    up_ref[half:] += left_ref[2 * capacity :]


def spread_kernel(home_ref, out_ref):
    groups, _, lane_count = home_ref.shape
    half = groups // 2
    home = jnp.sum(home_ref[...].reshape(2, half, lane_count), axis=1)
    out_ref[...] = jnp.broadcast_to(home[None], out_ref.shape)


def output_kernel(own_ref, down_ref, up_ref, gate_ref, gate_pre_ref, up_pre_ref, *outs):
    grad_gate_ref, grad_up_ref = outs
    hidden_grad = own_ref[...] + down_ref[...] + up_ref[...]
    gate_pre = gate_pre_ref[...].astype(F32)
    up_pre = up_pre_ref[...].astype(F32)
    sigmoid_gate = jax.nn.sigmoid(gate_pre)
    scaled = gate_ref[...] * hidden_grad
    grad_up_ref[...] = (scaled * gate_pre * sigmoid_gate).astype(BF16)
    grad_gate_ref[...] = (
        scaled * up_pre * sigmoid_gate * (1.0 + gate_pre * (1.0 - sigmoid_gate))
    ).astype(BF16)


def collect_kernel(terms_ref, routes_ref, slots_ref, out_ref):
    shard_count, experts, halves, lane_count = terms_ref.shape
    route_count, tok_count = routes_ref.shape
    table = terms_ref[0]
    for s in range(1, shard_count):
        table += terms_ref[s]
    routes = routes_ref[...]
    place = routes // EXP_GRP * SLOTS + slots_ref[...]
    places = jnp.concatenate([place[k : k + 1, :] for k in range(route_count)], axis=1)
    picked = jnp.zeros((experts, route_count * tok_count), F32)
    for h in range(halves):
        rest = table[:, h, :]
        parts = []
        for _ in range(3):
            part = rest.astype(BF16)
            parts.append(part)
            rest = rest - part.astype(F32)
        hit = rows((lane_count, route_count * tok_count)) + h * lane_count == places
        every = jnp.dot(
            jnp.concatenate(parts, axis=0),
            jnp.where(hit, 1.0, 0.0).astype(BF16),
            preferred_element_type=F32,
        )
        for i in range(3):
            picked += every[i * experts : (i + 1) * experts]
    for k in range(route_count):
        own = rows((experts, tok_count)) == routes[k : k + 1, :] % EXP_GRP
        column = picked[:, k * tok_count : (k + 1) * tok_count]
        out_ref[k : k + 1, :] = jnp.sum(jnp.where(own, column, 0.0), axis=0, keepdims=True)


VMEM = pl.BlockSpec(memory_space=pltpu.VMEM)
SMEM = pl.BlockSpec(memory_space=pltpu.SMEM)


def call(kernel, specs, out_shape, *args, limit=24 << 20):
    return pl.pallas_call(
        kernel,
        in_specs=specs,
        out_specs=jax.tree.map(lambda _: VMEM, out_shape),
        out_shape=out_shape,
        compiler_params=pltpu.CompilerParams(vmem_limit_bytes=limit),
    )(*args)


def shards(grad_out, routes, slots, gates, w_down, saved_gate, saved_up):
    shape = jax.ShapeDtypeStruct
    groups, shard_count, parts = (lax.axis_size(a) for a in ("group", "y", "xc"))
    capacity, lane_count = saved_gate.shape[1:]
    group = lax.axis_index("group").astype(jnp.int32)
    shard = lax.axis_index("y").astype(jnp.int32)
    column = shape((capacity, lane_count), F32)

    send, hidden = call(
        dispatch_kernel,
        [VMEM] * 6,
        (shape((groups * parts, SLOTS, lane_count), BF16), column),
        grad_out.T,
        routes.T,
        slots.T,
        gates.T,
        saved_gate[0],
        saved_up[0],
        limit=LARGE,
    )
    expert_rows = lax.all_to_all(send, ("group", "xc"), 0, 0, tiled=True)

    same = lax.all_gather(
        hidden, "y", axis_index_groups=[list(range(p, shard_count, 2)) for p in (0, 1)]
    )
    quads = shard_count // 2
    other = lax.ppermute(same, "y", [(i, i ^ 1) for i in range(shard_count)])
    send_shape = shape((2 * capacity + capacity // 2, lane_count), F32)
    right, left, keep, gate_rows, base = call(
        matmul_kernel,
        [SMEM] + [VMEM] * 3,
        (send_shape, send_shape, shape((3 * capacity, lane_count), F32), column, column),
        shard[None],
        expert_rows.reshape(groups, parts, SLOTS, lane_count),
        w_down[0],
        same,
        limit=24 << 20,
    )
    terms = call(
        terms_kernel,
        [SMEM] * 2 + [VMEM] * 5,
        shape((groups, 1, lane_count), F32),
        group[None],
        shard[None],
        right,
        left,
        keep,
        other,
        base,
        limit=24 << 20,
    )

    def moved(array, by):
        return lax.ppermute(
            array, "y", [(i, (i + by) % shard_count) for i in range(shard_count)]
        )

    from_left, from_right = moved(right, 1), moved(left, -1)
    home = lax.all_to_all(terms, "group", 0, 0, tiled=True)
    own, down, up = call(
        middle_kernel, [VMEM] * 3, (column,) * 3, from_left, from_right, keep
    )
    from_above, from_below = moved(down, -3), moved(up, 3)
    spread = call(
        spread_kernel, [VMEM], shape((shard_count * parts, 2, lane_count), F32), home
    )
    every_term = lax.all_to_all(spread, ("y", "xc"), 0, 0, tiled=True)
    out = shape((capacity, lane_count), BF16)
    grad_gate, grad_up = call(
        output_kernel,
        [VMEM] * 6,
        (out, out),
        own,
        from_above,
        from_below,
        gate_rows,
        saved_gate[0],
        saved_up[0],
    )
    every_term, grad_gate, grad_up = lax.optimization_barrier((every_term, grad_gate, grad_up))
    grad_gates = call(
        collect_kernel,
        [VMEM] * 3,
        shape(routes.shape[::-1], F32),
        every_term.reshape(shard_count, parts, 2, lane_count),
        routes.T,
        slots.T,
    )
    return (grad_gate[None], grad_up[None], grad_gates.T)


def solution(mesh):
    fine = Mesh(mesh.devices.reshape(mesh.shape["group"], -1, EXP_GRP), ("group", "y", "xc"))
    local, device = ("y", "xc"), ("group", "y", "xc")
    return jax.shard_map(
        shards,
        mesh=fine,
        in_specs=(
            P("group", local),
            P("group", None),
            P("group", None),
            P("group", None),
            P(device, None, None),
            P(device, None, None),
            P(device, None, None),
        ),
        out_specs=(P(device, None, None), P(device, None, None), P("group", None)),
        check_vma=False,
    )
```

```python
import jax
import jax.numpy as jnp
from jax import lax
from jax.experimental import pallas as pl
from jax.experimental.pallas import tpu as pltpu
from jax.sharding import Mesh, PartitionSpec as P

EXP_GRP = 8
SLOTS = 16
NT = (((1,), (1,)), ((), ()))
F32 = jnp.float32
LARGE = 56 << 20
BF16 = jnp.bfloat16


def lanes(shape):
    return lax.broadcasted_iota(jnp.int32, shape, len(shape) - 1)


def rows(shape):
    return lax.broadcasted_iota(jnp.int32, shape, 0)


def dispatch_kernel(
    tokens_ref, routes_ref, slots_ref, gates_ref, gate_pre_ref, up_pre_ref, out_ref, hidden_ref
):
    col_width, tok_count = tokens_ref.shape
    lane_count = out_ref.shape[2]
    place = routes_ref[...] * SLOTS + slots_ref[...]
    gates = gates_ref[...].astype(F32)
    spare = (lane_count - col_width, tok_count)
    features = jnp.concatenate([tokens_ref[...], jnp.zeros(spare, BF16)], axis=0)
    marks = jnp.where(rows((lane_count, tok_count)) == col_width, 1.0, 0.0).astype(BF16)
    source = jnp.concatenate([features, marks], axis=1)
    chunk = 256
    for start in range(0, out_ref.shape[0] * SLOTS, chunk):
        row_ids = rows((chunk, tok_count)) + start
        gate = jnp.zeros((chunk, tok_count), F32)
        for k in range(place.shape[0]):
            gate = jnp.where(row_ids == place[k : k + 1, :], gates[k : k + 1, :], gate)
        pick = jnp.where(gate > 0.0, 1.0, 0.0)
        both = jnp.concatenate([pick.astype(BF16), gate.astype(BF16)], axis=1)
        block = lax.dot_general(both, source, NT, preferred_element_type=F32)
        out_ref[start // SLOTS : (start + chunk) // SLOTS] = block.astype(BF16).reshape(
            chunk // SLOTS, SLOTS, lane_count
        )
    gate_pre = gate_pre_ref[...].astype(F32)
    hidden_ref[...] = gate_pre * jax.nn.sigmoid(gate_pre) * up_pre_ref[...].astype(F32)


def matmul_kernel(
    shard_ref, rows_ref, w_ref, same_ref, right_ref, left_ref, keep_ref, gate_ref, base_ref
):
    groups, parts, _, lane_count = rows_ref.shape
    capacity = groups * SLOTS
    col_width = w_ref.shape[1] // parts
    count = w_ref.shape[0] // lane_count
    shard = shard_ref[0]
    half = capacity // 2
    low, high = slice(0, half), slice(half, capacity)
    every, near = slice(0, capacity), slice(capacity, 2 * capacity)
    last, spare = slice(2 * capacity, 3 * capacity), slice(2 * capacity, 2 * capacity + half)
    pairs = (
        ((1, ((every, right_ref, every),)), (count - 1, ((every, left_ref, every),))),
        ((count - 2, ((every, right_ref, near),)), (2, ((every, left_ref, near),))),
        (
            (4, ((high, right_ref, spare), (low, left_ref, spare))),
            (0, ((every, keep_ref, every),)),
        ),
        ((count - 3, ((every, keep_ref, near),)), (3, ((every, keep_ref, last),))),
    )
    blocks = [rows_ref[:, e].reshape(capacity, lane_count) for e in range(parts)]
    x = jnp.concatenate([b[:, :col_width] for b in blocks], axis=1)
    terms = jnp.zeros((capacity, lane_count), F32)
    for pair in pairs:
        units = [(shard + offset) % count for offset, _ in pair]
        firsts = [pl.multiple_of(unit * lane_count, lane_count) for unit in units]
        w = jnp.concatenate([w_ref[pl.ds(first, lane_count), :] for first in firsts], axis=0)
        both = lax.dot_general(x, w, NT, preferred_element_type=F32)
        for i, (offset, targets) in enumerate(pair):
            part = both[:, i * lane_count : (i + 1) * lane_count]
            for span, target_ref, to in targets:
                target_ref[to] = part[span]
            if offset % 2 == 0:
                terms += part * same_ref[units[i] // 2]
    base_ref[...] = terms
    gate = jnp.where(lanes((capacity, lane_count)) == col_width, blocks[0].astype(F32), 0.0)
    gate_ref[...] = jnp.broadcast_to(
        jnp.sum(gate, axis=1, keepdims=True), (capacity, lane_count)
    )


def terms_kernel(
    group_ref, shard_ref, right_in, left_in, keep_ref, other_ref, base_ref, term_ref, odd_ref, sems
):
    capacity, lane_count = base_ref.shape
    groups = term_ref.shape[0]
    count = 2 * other_ref.shape[0]
    group, shard = group_ref[0], shard_ref[0]
    copies = [
        pltpu.make_async_copy(part.at[:capacity], odd_ref.at[i], sems.at[i])
        for i, part in enumerate((right_in, left_in))
    ]
    for copy in copies:
        copy.start()

    def product(offset, part):
        return part * other_ref[(shard + offset) % count // 2]

    terms = base_ref[...]
    terms += product(count - 3, keep_ref[capacity : 2 * capacity])
    terms += product(3, keep_ref[2 * capacity :])
    for copy in copies:
        copy.wait()
    terms += product(1, odd_ref[0])
    terms += product(count - 1, odd_ref[1])
    total = jnp.sum(terms, axis=1, keepdims=True)
    row_ids, lane_ids = rows((capacity, lane_count)), lanes((capacity, lane_count))
    hit = lane_ids == group % (lane_count // SLOTS) * SLOTS + row_ids % SLOTS
    term_ref[...] = jnp.sum(
        jnp.where(hit, total, 0.0).reshape(groups, SLOTS, lane_count), axis=1, keepdims=True
    )


def middle_kernel(left_ref, right_ref, keep_ref, own_ref, down_ref, up_ref):
    capacity = down_ref.shape[0]
    half = capacity // 2
    near = slice(capacity, 2 * capacity)
    own_ref[...] = keep_ref[:capacity] + left_ref[:capacity] + right_ref[:capacity]
    down_ref[...] = keep_ref[near] + left_ref[near]
    down_ref[:half] += right_ref[2 * capacity :]
    up_ref[...] = keep_ref[2 * capacity :] + right_ref[near]
    up_ref[half:] += left_ref[2 * capacity :]


def spread_kernel(home_ref, out_ref):
    groups, _, lane_count = home_ref.shape
    half = groups // 2
    home = jnp.sum(home_ref[...].reshape(2, half, lane_count), axis=1)
    out_ref[...] = jnp.broadcast_to(home[None], out_ref.shape)


def output_kernel(own_ref, down_ref, up_ref, gate_ref, gate_pre_ref, up_pre_ref, *outs):
    grad_gate_ref, grad_up_ref = outs
    hidden_grad = own_ref[...] + down_ref[...] + up_ref[...]
    gate_pre = gate_pre_ref[...].astype(F32)
    up_pre = up_pre_ref[...].astype(F32)
    sigmoid_gate = jax.nn.sigmoid(gate_pre)
    scaled = gate_ref[...] * hidden_grad
    grad_up_ref[...] = (scaled * gate_pre * sigmoid_gate).astype(BF16)
    grad_gate_ref[...] = (
        scaled * up_pre * sigmoid_gate * (1.0 + gate_pre * (1.0 - sigmoid_gate))
    ).astype(BF16)


def collect_kernel(terms_ref, routes_ref, slots_ref, out_ref):
    shard_count, experts, halves, lane_count = terms_ref.shape
    route_count, tok_count = routes_ref.shape
    table = terms_ref[0]
    for s in range(1, shard_count):
        table += terms_ref[s]
    routes = routes_ref[...]
    place = routes // EXP_GRP * SLOTS + slots_ref[...]
    places = jnp.concatenate([place[k : k + 1, :] for k in range(route_count)], axis=1)
    picked = jnp.zeros((experts, route_count * tok_count), F32)
    for h in range(halves):
        rest = table[:, h, :]
        parts = []
        for _ in range(3):
            part = rest.astype(BF16)
            parts.append(part)
            rest = rest - part.astype(F32)
        hit = rows((lane_count, route_count * tok_count)) + h * lane_count == places
        every = jnp.dot(
            jnp.concatenate(parts, axis=0),
            jnp.where(hit, 1.0, 0.0).astype(BF16),
            preferred_element_type=F32,
        )
        for i in range(3):
            picked += every[i * experts : (i + 1) * experts]
    for k in range(route_count):
        own = rows((experts, tok_count)) == routes[k : k + 1, :] % EXP_GRP
        column = picked[:, k * tok_count : (k + 1) * tok_count]
        out_ref[k : k + 1, :] = jnp.sum(jnp.where(own, column, 0.0), axis=0, keepdims=True)


VMEM = pl.BlockSpec(memory_space=pltpu.VMEM)
SMEM = pl.BlockSpec(memory_space=pltpu.SMEM)
HBM = pl.BlockSpec(memory_space=pltpu.HBM)


def call(kernel, specs, out_shape, *args, limit=24 << 20):
    return pl.pallas_call(
        kernel,
        in_specs=specs,
        out_specs=jax.tree.map(lambda _: VMEM, out_shape),
        out_shape=out_shape,
        compiler_params=pltpu.CompilerParams(vmem_limit_bytes=limit),
    )(*args)


def shards(grad_out, routes, slots, gates, w_down, saved_gate, saved_up):
    shape = jax.ShapeDtypeStruct
    groups, shard_count, parts = (lax.axis_size(a) for a in ("group", "y", "xc"))
    capacity, lane_count = saved_gate.shape[1:]
    group = lax.axis_index("group").astype(jnp.int32)
    shard = lax.axis_index("y").astype(jnp.int32)
    column = shape((capacity, lane_count), F32)

    send, hidden = call(
        dispatch_kernel,
        [VMEM] * 6,
        (shape((groups * parts, SLOTS, lane_count), BF16), column),
        grad_out.T,
        routes.T,
        slots.T,
        gates.T,
        saved_gate[0],
        saved_up[0],
        limit=LARGE,
    )
    expert_rows = lax.all_to_all(send, ("group", "xc"), 0, 0, tiled=True)

    same = lax.all_gather(
        hidden, "y", axis_index_groups=[list(range(p, shard_count, 2)) for p in (0, 1)]
    )
    quads = shard_count // 2
    other = lax.ppermute(same, "y", [(i, i ^ 1) for i in range(shard_count)])
    send_shape = shape((2 * capacity + capacity // 2, lane_count), F32)
    right, left, keep, gate_rows, base = call(
        matmul_kernel,
        [SMEM] + [VMEM] * 3,
        (send_shape, send_shape, shape((3 * capacity, lane_count), F32), column, column),
        shard[None],
        expert_rows.reshape(groups, parts, SLOTS, lane_count),
        w_down[0],
        same,
        limit=24 << 20,
    )
    terms = pl.pallas_call(
        terms_kernel,
        in_specs=[SMEM] * 2 + [HBM] * 2 + [VMEM] * 3,
        out_specs=VMEM,
        out_shape=shape((groups, 1, lane_count), F32),
        scratch_shapes=[
            pltpu.VMEM((2, capacity, lane_count), F32),
            pltpu.SemaphoreType.DMA((2,)),
        ],
        compiler_params=pltpu.CompilerParams(vmem_limit_bytes=24 << 20),
    )(group[None], shard[None], right, left, keep, other, base)

    def moved(array, by):
        return lax.ppermute(
            array, "y", [(i, (i + by) % shard_count) for i in range(shard_count)]
        )

    from_left, from_right = moved(right, 1), moved(left, -1)
    home = lax.all_to_all(terms, "group", 0, 0, tiled=True)
    own, down, up = call(
        middle_kernel, [VMEM] * 3, (column,) * 3, from_left, from_right, keep
    )
    from_above, from_below = moved(down, -3), moved(up, 3)
    spread = call(
        spread_kernel, [VMEM], shape((shard_count * parts, 2, lane_count), F32), home
    )
    every_term = lax.all_to_all(spread, ("y", "xc"), 0, 0, tiled=True)
    out = shape((capacity, lane_count), BF16)
    grad_gate, grad_up = call(
        output_kernel,
        [VMEM] * 6,
        (out, out),
        own,
        from_above,
        from_below,
        gate_rows,
        saved_gate[0],
        saved_up[0],
    )
    every_term, grad_gate, grad_up = lax.optimization_barrier((every_term, grad_gate, grad_up))
    grad_gates = call(
        collect_kernel,
        [VMEM] * 3,
        shape(routes.shape[::-1], F32),
        every_term.reshape(shard_count, parts, 2, lane_count),
        routes.T,
        slots.T,
    )
    return (grad_gate[None], grad_up[None], grad_gates.T)


def solution(mesh):
    fine = Mesh(mesh.devices.reshape(mesh.shape["group"], -1, EXP_GRP), ("group", "y", "xc"))
    local, device = ("y", "xc"), ("group", "y", "xc")
    return jax.shard_map(
        shards,
        mesh=fine,
        in_specs=(
            P("group", local),
            P("group", None),
            P("group", None),
            P("group", None),
            P(device, None, None),
            P(device, None, None),
            P(device, None, None),
        ),
        out_specs=(P(device, None, None), P(device, None, None), P("group", None)),
        check_vma=False,
    )
```

```python
import jax
import jax.numpy as jnp
from jax import lax
from jax.experimental import pallas as pl
from jax.experimental.pallas import tpu as pltpu
from jax.sharding import Mesh, PartitionSpec as P

EXP_GRP = 8
SLOTS = 16
NT = (((1,), (1,)), ((), ()))
F32 = jnp.float32
LARGE = 56 << 20
BF16 = jnp.bfloat16


def lanes(shape):
    return lax.broadcasted_iota(jnp.int32, shape, len(shape) - 1)


def rows(shape):
    return lax.broadcasted_iota(jnp.int32, shape, 0)


def dispatch_kernel(
    tokens_ref, routes_ref, slots_ref, gates_ref, gate_pre_ref, up_pre_ref, out_ref, hidden_ref
):
    col_width, tok_count = tokens_ref.shape
    lane_count = out_ref.shape[2]
    place = routes_ref[...] * SLOTS + slots_ref[...]
    gates = gates_ref[...].astype(F32)
    spare = (lane_count - col_width, tok_count)
    features = jnp.concatenate([tokens_ref[...], jnp.zeros(spare, BF16)], axis=0)
    marks = jnp.where(rows((lane_count, tok_count)) == col_width, 1.0, 0.0).astype(BF16)
    source = jnp.concatenate([features, marks], axis=1)
    chunk = 256
    for start in range(0, out_ref.shape[0] * SLOTS, chunk):
        row_ids = rows((chunk, tok_count)) + start
        pick = jnp.zeros((chunk, tok_count), F32)
        gate = jnp.zeros((chunk, tok_count), F32)
        for k in range(place.shape[0]):
            hit = row_ids == place[k : k + 1, :]
            pick = jnp.where(hit, 1.0, pick)
            gate = jnp.where(hit, gates[k : k + 1, :], gate)
        both = jnp.concatenate([pick.astype(BF16), gate.astype(BF16)], axis=1)
        block = lax.dot_general(both, source, NT, preferred_element_type=F32)
        out_ref[start // SLOTS : (start + chunk) // SLOTS] = block.astype(BF16).reshape(
            chunk // SLOTS, SLOTS, lane_count
        )
    gate_pre = gate_pre_ref[...].astype(F32)
    hidden_ref[...] = gate_pre * jax.nn.sigmoid(gate_pre) * up_pre_ref[...].astype(F32)


def matmul_kernel(
    shard_ref, rows_ref, w_ref, same_ref, right_ref, left_ref, keep_ref, gate_ref, base_ref
):
    groups, parts, _, lane_count = rows_ref.shape
    capacity = groups * SLOTS
    col_width = w_ref.shape[1] // parts
    count = w_ref.shape[0] // lane_count
    shard = shard_ref[0]
    half = capacity // 2
    low, high = slice(0, half), slice(half, capacity)
    every, near = slice(0, capacity), slice(capacity, 2 * capacity)
    last, spare = slice(2 * capacity, 3 * capacity), slice(2 * capacity, 2 * capacity + half)
    pairs = (
        ((1, ((every, right_ref, every),)), (count - 1, ((every, left_ref, every),))),
        ((count - 2, ((every, right_ref, near),)), (2, ((every, left_ref, near),))),
        (
            (4, ((high, right_ref, spare), (low, left_ref, spare))),
            (0, ((every, keep_ref, every),)),
        ),
        ((count - 3, ((every, keep_ref, near),)), (3, ((every, keep_ref, last),))),
    )
    blocks = [rows_ref[:, e].reshape(capacity, lane_count) for e in range(parts)]
    x = jnp.concatenate([b[:, :col_width] for b in blocks], axis=1)
    terms = jnp.zeros((capacity, lane_count), F32)
    for pair in pairs:
        units = [(shard + offset) % count for offset, _ in pair]
        firsts = [pl.multiple_of(unit * lane_count, lane_count) for unit in units]
        w = jnp.concatenate([w_ref[pl.ds(first, lane_count), :] for first in firsts], axis=0)
        both = lax.dot_general(x, w, NT, preferred_element_type=F32)
        for i, (offset, targets) in enumerate(pair):
            part = both[:, i * lane_count : (i + 1) * lane_count]
            for span, target_ref, to in targets:
                target_ref[to] = part[span]
            if offset % 2 == 0:
                terms += part * same_ref[units[i] // 2]
    base_ref[...] = terms
    gate = jnp.where(lanes((capacity, lane_count)) == col_width, blocks[0].astype(F32), 0.0)
    gate_ref[...] = jnp.broadcast_to(
        jnp.sum(gate, axis=1, keepdims=True), (capacity, lane_count)
    )


def terms_kernel(
    group_ref, shard_ref, right_ref, left_ref, keep_ref, other_ref, base_ref, term_ref
):
    capacity, lane_count = base_ref.shape
    groups = term_ref.shape[0]
    count = 2 * other_ref.shape[0]
    group, shard = group_ref[0], shard_ref[0]
    terms = base_ref[...]
    for offset, part_ref, first in (
        (1, right_ref, 0),
        (count - 1, left_ref, 0),
        (count - 3, keep_ref, capacity),
        (3, keep_ref, 2 * capacity),
    ):
        unit = (shard + offset) % count
        terms += part_ref[first : first + capacity] * other_ref[unit // 2]
    total = jnp.sum(terms, axis=1, keepdims=True)
    row_ids, lane_ids = rows((capacity, lane_count)), lanes((capacity, lane_count))
    hit = lane_ids == group % (lane_count // SLOTS) * SLOTS + row_ids % SLOTS
    term_ref[...] = jnp.sum(
        jnp.where(hit, total, 0.0).reshape(groups, SLOTS, lane_count), axis=1, keepdims=True
    )


def middle_kernel(left_ref, right_ref, keep_ref, own_ref, down_ref, up_ref):
    capacity = down_ref.shape[0]
    half = capacity // 2
    near = slice(capacity, 2 * capacity)
    own_ref[...] = keep_ref[:capacity] + left_ref[:capacity] + right_ref[:capacity]
    down_ref[...] = keep_ref[near] + left_ref[near]
    down_ref[:half] += right_ref[2 * capacity :]
    up_ref[...] = keep_ref[2 * capacity :] + right_ref[near]
    up_ref[half:] += left_ref[2 * capacity :]


def spread_kernel(home_ref, out_ref):
    groups, _, lane_count = home_ref.shape
    half = groups // 2
    home = jnp.sum(home_ref[...].reshape(2, half, lane_count), axis=1)
    out_ref[...] = jnp.broadcast_to(home[None], out_ref.shape)


def output_kernel(own_ref, down_ref, up_ref, gate_ref, gate_pre_ref, up_pre_ref, *outs):
    grad_gate_ref, grad_up_ref = outs
    hidden_grad = own_ref[...] + down_ref[...] + up_ref[...]
    gate_pre = gate_pre_ref[...].astype(F32)
    up_pre = up_pre_ref[...].astype(F32)
    sigmoid_gate = jax.nn.sigmoid(gate_pre)
    scaled = gate_ref[...] * hidden_grad
    grad_up_ref[...] = (scaled * gate_pre * sigmoid_gate).astype(BF16)
    grad_gate_ref[...] = (
        scaled * up_pre * sigmoid_gate * (1.0 + gate_pre * (1.0 - sigmoid_gate))
    ).astype(BF16)


def collect_kernel(terms_ref, routes_ref, slots_ref, out_ref):
    shard_count, experts, halves, lane_count = terms_ref.shape
    route_count, tok_count = routes_ref.shape
    table = terms_ref[0]
    for s in range(1, shard_count):
        table += terms_ref[s]
    routes = routes_ref[...]
    place = routes // EXP_GRP * SLOTS + slots_ref[...]
    places = jnp.concatenate([place[k : k + 1, :] for k in range(route_count)], axis=1)
    picked = jnp.zeros((experts, route_count * tok_count), F32)
    for h in range(halves):
        rest = table[:, h, :]
        parts = []
        for _ in range(3):
            part = rest.astype(BF16)
            parts.append(part)
            rest = rest - part.astype(F32)
        hit = rows((lane_count, route_count * tok_count)) + h * lane_count == places
        every = jnp.dot(
            jnp.concatenate(parts, axis=0),
            jnp.where(hit, 1.0, 0.0).astype(BF16),
            preferred_element_type=F32,
        )
        for i in range(3):
            picked += every[i * experts : (i + 1) * experts]
    for k in range(route_count):
        own = rows((experts, tok_count)) == routes[k : k + 1, :] % EXP_GRP
        column = picked[:, k * tok_count : (k + 1) * tok_count]
        out_ref[k : k + 1, :] = jnp.sum(jnp.where(own, column, 0.0), axis=0, keepdims=True)


VMEM = pl.BlockSpec(memory_space=pltpu.VMEM)
SMEM = pl.BlockSpec(memory_space=pltpu.SMEM)


def call(kernel, specs, out_shape, *args, limit=24 << 20):
    return pl.pallas_call(
        kernel,
        in_specs=specs,
        out_specs=jax.tree.map(lambda _: VMEM, out_shape),
        out_shape=out_shape,
        compiler_params=pltpu.CompilerParams(vmem_limit_bytes=limit),
    )(*args)


def shards(grad_out, routes, slots, gates, w_down, saved_gate, saved_up):
    shape = jax.ShapeDtypeStruct
    groups, shard_count, parts = (lax.axis_size(a) for a in ("group", "y", "xc"))
    capacity, lane_count = saved_gate.shape[1:]
    group = lax.axis_index("group").astype(jnp.int32)
    shard = lax.axis_index("y").astype(jnp.int32)
    column = shape((capacity, lane_count), F32)

    send, hidden = call(
        dispatch_kernel,
        [VMEM] * 6,
        (shape((groups * parts, SLOTS, lane_count), BF16), column),
        grad_out.T,
        routes.T,
        slots.T,
        gates.T,
        saved_gate[0],
        saved_up[0],
        limit=LARGE,
    )
    expert_rows = lax.all_to_all(send, ("group", "xc"), 0, 0, tiled=True)

    same = lax.all_gather(
        hidden, "y", axis_index_groups=[list(range(p, shard_count, 2)) for p in (0, 1)]
    )
    quads = shard_count // 2
    other = lax.ppermute(same, "y", [(i, i ^ 1) for i in range(shard_count)])
    send_shape = shape((2 * capacity + capacity // 2, lane_count), F32)
    right, left, keep, gate_rows, base = call(
        matmul_kernel,
        [SMEM] + [VMEM] * 3,
        (send_shape, send_shape, shape((3 * capacity, lane_count), F32), column, column),
        shard[None],
        expert_rows.reshape(groups, parts, SLOTS, lane_count),
        w_down[0],
        same,
        limit=24 << 20,
    )
    terms = call(
        terms_kernel,
        [SMEM] * 2 + [VMEM] * 5,
        shape((groups, 1, lane_count), F32),
        group[None],
        shard[None],
        right,
        left,
        keep,
        other,
        base,
        limit=24 << 20,
    )

    def moved(array, by):
        return lax.ppermute(
            array, "y", [(i, (i + by) % shard_count) for i in range(shard_count)]
        )

    from_left, from_right = moved(right, 1), moved(left, -1)
    home = lax.all_to_all(terms, "group", 0, 0, tiled=True)
    own, down, up = call(
        middle_kernel, [VMEM] * 3, (column,) * 3, from_left, from_right, keep
    )
    from_above, from_below = moved(down, -3), moved(up, 3)
    spread = call(
        spread_kernel, [VMEM], shape((shard_count * parts, 2, lane_count), F32), home
    )
    every_term = lax.all_to_all(spread, ("y", "xc"), 0, 0, tiled=True)
    out = shape((capacity, lane_count), BF16)
    grad_gate, grad_up = call(
        output_kernel,
        [VMEM] * 6,
        (out, out),
        own,
        from_above,
        from_below,
        gate_rows,
        saved_gate[0],
        saved_up[0],
    )
    every_term, grad_gate, grad_up = lax.optimization_barrier((every_term, grad_gate, grad_up))
    grad_gates = call(
        collect_kernel,
        [VMEM] * 3,
        shape(routes.shape[::-1], F32),
        every_term.reshape(shard_count, parts, 2, lane_count),
        routes.T,
        slots.T,
    )
    return (grad_gate[None], grad_up[None], grad_gates.T)


def solution(mesh):
    fine = Mesh(mesh.devices.reshape(mesh.shape["group"], -1, EXP_GRP), ("group", "y", "xc"))
    local, device = ("y", "xc"), ("group", "y", "xc")
    return jax.shard_map(
        shards,
        mesh=fine,
        in_specs=(
            P("group", local),
            P("group", None),
            P("group", None),
            P("group", None),
            P(device, None, None),
            P(device, None, None),
            P(device, None, None),
        ),
        out_specs=(P(device, None, None), P(device, None, None), P("group", None)),
        check_vma=False,
    )
```
